512 devices in a mesh: grp: 32 (over y, x, core), seq: 16 (over z).
Axes of the slice: x: 4, y: 4, z: 16, core: 2. Of those that a mesh axis runs over, the one named last changes fastest.
Arguments:
- query_sp: bfloat16 [32, 16, 256, 1536], P('grp', 'seq'), may hold values from -80 to 80
- key_sp: bfloat16 [32, 16, 256, 1536], P('grp', 'seq'), may hold values from -8 to 8
- value_sp: bfloat16 [32, 16, 256, 1536], P('grp', 'seq'), may hold values from -6 to 6
- query_tm: bfloat16 [32, 16, 256, 1536], P('grp', 'seq'), may hold values from -80 to 80
- key_tm: bfloat16 [32, 16, 256, 1536], P('grp', 'seq'), may hold values from -8 to 8
- clip_shape: int32 [32, 2], replicated, may hold values from 1 to 256, as said below
- route: int32 [32], replicated, may hold values from 0 to 31
Outputs:
- mixed: bfloat16 [32, 16, 256, 1536], P('grp', 'seq')
The draws below stay inside these ranges and needn't reach their ends.
Inputs may be any that keep to these rules, and one draw needn't show every extreme that they name: `clip_shape`: each entry of column 0 is one of 4, 8, 16; each entry of column 1 is a multiple of 64 up to 256; clip 0 has 16 frames and 256 patches.
All inputs are finite; a program needn't handle non-finite values.
Results may differ from the reference program's by a relative error of at most 0.015.
Values may be sent and summed in bfloat16 or wider, within the bound.
A program may use at most 64 MiB of HBM per device.

```python
import jax
import jax.numpy as jnp
from jax import lax

HEADS = 12
HD = 128
PA = 256
FR = 16
CLIPS = 32
SECTIONS = 5


def paired_spatial(key):
    key_query, key_keys = jax.random.split(jax.random.fold_in(key, 101))
    shape = (CLIPS, FR, PA, HEADS * HD)
    queries = jax.random.normal(key_query, shape, jnp.float32)
    keys = jax.random.normal(key_keys, shape, jnp.float32)
    return (jnp.clip(queries, -80.0, 80.0), jnp.clip(keys, -8.0, 8.0))


def paired_temporal(key):
    key_query, key_keys = jax.random.split(jax.random.fold_in(key, 202))
    shape = (CLIPS, FR, PA, HEADS * HD)
    queries = jax.random.normal(key_query, shape, jnp.float32)
    keys = jax.random.normal(key_keys, shape, jnp.float32)
    return (jnp.clip(queries, -80.0, 80.0), jnp.clip(keys, -8.0, 8.0))


def draw_query_sp(key, part):
    return paired_spatial(key)[0].astype(jnp.bfloat16)


def draw_key_sp(key, part):
    return paired_spatial(key)[1].astype(jnp.bfloat16)


def draw_query_tm(key, part):
    return paired_temporal(key)[0].astype(jnp.bfloat16)


def draw_key_tm(key, part):
    return paired_temporal(key)[1].astype(jnp.bfloat16)


def draw_clip_shape(key, part):
    key = jax.random.fold_in(key, 5)
    key_frames, key_patches = jax.random.split(key)
    frames = FR // 4 * jnp.left_shift(1, jax.random.randint(key_frames, (CLIPS,), 0, 3))
    patches = PA // 4 * jax.random.randint(key_patches, (CLIPS,), 1, 5)
    frames = frames.at[0].set(FR)
    patches = patches.at[0].set(PA)
    return jnp.stack([frames, patches], axis=1).astype(jnp.int32)


def touch_ends(drawn, rng, least, largest):
    shape = drawn.shape
    index_at = [jax.random.randint(jax.random.fold_in(rng, axis), (), 0, shape[axis]) for axis in range(len(shape))]
    drawn = drawn.at[tuple(index_at)].set(least)
    longest = shape.index(max(shape))
    index_at[longest] = (index_at[longest] + 1) % shape[longest]
    return drawn.at[tuple(index_at)].set(largest)


def block_scale(own_key, dims, shards, smallest, high):
    def one(axis_at, parts):
        heights = jax.random.uniform(jax.random.fold_in(jax.random.fold_in(own_key, 6), axis_at), (parts,), jnp.float32, smallest / len(shards), high / len(shards))
        return jnp.repeat(jnp.exp(heights), dims[axis_at] // parts).reshape((-1,) + (1,) * (len(dims) - axis_at - 1))

    gain = one(*shards[0])
    for cut in shards[1:]:
        gain = gain * one(*cut)
    return gain


def bell_draw(rng, extent, scale, bound, cuts=(), kind=jnp.bfloat16):
    array = jax.random.normal(rng, extent, jnp.float32) * scale
    if len(cuts) > 0:
        array = block_scale(rng, extent, cuts, -0.22, 0.18) * array
    return jnp.clip(array, min=-bound, max=bound).astype(kind)


def setup_inputs(seed: int = 0) -> dict:
    arg_keys = jax.random.split(jax.random.key(seed), 8)
    query_sp = draw_query_sp(jax.random.fold_in(arg_keys[7], 71), 0)
    key_sp = draw_key_sp(jax.random.fold_in(arg_keys[7], 71), 0)
    value_sp = bell_draw(arg_keys[2], (CLIPS, FR, PA, HEADS * HD), 1.0, 6.0, ((0, 32), (1, 16)))
    query_tm = draw_query_tm(jax.random.fold_in(arg_keys[7], 71), 0)
    key_tm = draw_key_tm(jax.random.fold_in(arg_keys[7], 71), 0)
    clip_shape = draw_clip_shape(jax.random.fold_in(arg_keys[7], 71), 0)
    route = touch_ends(jax.random.randint(arg_keys[6], (CLIPS,), 0, CLIPS), jax.random.fold_in(arg_keys[6], 1), 0, CLIPS - 1).astype(jnp.int32)
    return {"query_sp": query_sp, "key_sp": key_sp, "value_sp": value_sp, "query_tm": query_tm, "key_tm": key_tm, "clip_shape": clip_shape, "route": route}


def softmax_rows(scores):
    top = jnp.max(scores, axis=-1, keepdims=True)
    expo = jnp.exp(scores - top)
    return expo / jnp.sum(expo, axis=-1, keepdims=True)


def one_clip(items):
    query_sp, key_sp, value_sp, query_tm, key_tm, shape_row = items
    scale = HD ** -0.5
    frame_count = shape_row[0]
    patch_count = shape_row[1]
    frame_ids = jnp.arange(FR, dtype=jnp.int32)
    patch_ids = jnp.arange(PA, dtype=jnp.int32)
    valid = (frame_ids[:, None] < frame_count) & (patch_ids[None, :] < patch_count)
    shaped = (FR, PA, HEADS, HD)
    qsp = query_sp.reshape(shaped).astype(jnp.float32)
    ksp = key_sp.reshape(shaped).astype(jnp.float32)
    vsp = value_sp.reshape(shaped).astype(jnp.float32)
    scores = jnp.einsum('fphd,fqhd->fhpq', qsp, ksp) * scale
    scores = jnp.where(patch_ids[None, None, None, :] < patch_count, scores, -1e30)
    weights = softmax_rows(scores).astype(jnp.bfloat16)
    spatial = jnp.einsum('fhpq,fqhd->fphd', weights.astype(jnp.float32), vsp)
    spatial = jnp.where(valid[:, :, None, None], spatial, 0.0).astype(jnp.bfloat16)
    qtm = query_tm.reshape(shaped).astype(jnp.float32)
    ktm = key_tm.reshape(shaped).astype(jnp.float32)
    scores_tm = jnp.einsum('fphd,gphd->phfg', qtm, ktm) * scale
    scores_tm = jnp.where(frame_ids[None, None, None, :] < frame_count, scores_tm, -1e30)
    weights_tm = softmax_rows(scores_tm).astype(jnp.bfloat16)
    temporal = jnp.einsum('phfg,gphd->fphd', weights_tm.astype(jnp.float32), spatial.astype(jnp.float32))
    temporal = jnp.where(valid[:, :, None, None], temporal, 0.0).astype(jnp.bfloat16)
    return temporal.reshape(FR, PA, HEADS * HD)


def trace_anchor(route, count, sections):
    groups = jnp.arange(count, dtype=jnp.int32)
    anchor = groups
    for section in range(sections):
        partner = jnp.bitwise_xor(groups, 1 << section)
        lower = jnp.minimum(groups, partner)
        cross = jnp.bitwise_and(jnp.right_shift(route[lower], section), 1)
        anchor = jnp.where(cross == 1, anchor[partner], anchor)
    return anchor


def reference(query_sp, key_sp, value_sp, query_tm, key_tm, clip_shape, route):
    temporal = lax.map(one_clip, (query_sp, key_sp, value_sp, query_tm, key_tm, clip_shape))
    anchor = trace_anchor(route, CLIPS, SECTIONS)
    return jnp.take(temporal, anchor.astype(jnp.int32), axis=0)
```

```python
import functools

import jax
import jax.numpy as jnp
import numpy as np
from jax import lax
from jax.experimental import pallas as pl
from jax.experimental.pallas import tpu as pltpu
from jax.sharding import PartitionSpec as P

HD = 128
TILE = 16
MESH = pl.DeviceIdType.MESH
NEG = -1e30
PLANS = ((4, 4, 9), (5, 4, 9), (6, 4, 7))


def swapped(value, axis, bit):
    mask = 2**bit
    pairs = [(source, source ^ mask) for source in range(lax.axis_size(axis))]
    return lax.ppermute(value, axis, pairs)


def softmax_rows(scores):
    top = jnp.max(scores, axis=-1, keepdims=True)
    expo = jnp.exp(scores - top)
    return expo / jnp.sum(expo, axis=-1, keepdims=True)


def section_cross(route, group_idx, section):
    partner = jnp.bitwise_xor(group_idx, 1 << section)
    lower = jnp.minimum(group_idx, partner)
    return jnp.bitwise_and(jnp.right_shift(route[lower], section), 1) == 1


def general(query_sp, key_sp, value_sp, query_tm, key_tm, clip_shape, route):
    groups = lax.axis_size("grp")
    shards = lax.axis_size("seq")
    group_idx = lax.axis_index("grp")
    shard_idx = lax.axis_index("seq")
    sections = groups.bit_length() - 1
    frames_dev = query_sp.shape[1]
    patches = query_sp.shape[2]
    width = query_sp.shape[3]
    heads = width // HD
    frames = frames_dev * shards
    patches_dev = patches // shards
    scale = HD ** (-0.5)
    own_shape = clip_shape[group_idx]
    frame_ids = shard_idx * frames_dev + jnp.arange(frames_dev, dtype=jnp.int32)
    patch_all = jnp.arange(patches, dtype=jnp.int32)
    shaped = (frames_dev, patches, heads, HD)
    queries = query_sp[0].reshape(shaped)
    keys = key_sp[0].reshape(shaped)
    values = value_sp[0].reshape(shaped)
    scores = (
        jnp.einsum("fphd,fqhd->fhpq", queries, keys, preferred_element_type=jnp.float32) * scale
    )
    scores = jnp.where(patch_all[None, None, None, :] < own_shape[1], scores, NEG)
    weights = softmax_rows(scores).astype(jnp.bfloat16)
    spatial = jnp.einsum("fhpq,fqhd->fphd", weights, values, preferred_element_type=jnp.float32)
    valid_sp = (frame_ids[:, None] < own_shape[0]) & (patch_all[None, :] < own_shape[1])
    spatial = jnp.where(valid_sp[:, :, None, None], spatial, 0.0).astype(jnp.bfloat16)
    spatial = spatial.reshape(1, frames_dev, patches, width)
    query_pt, key_pt, spatial_pt = (
        lax.all_to_all(query_tm, "seq", split_axis=2, concat_axis=1, tiled=True),
        lax.all_to_all(key_tm, "seq", split_axis=2, concat_axis=1, tiled=True),
        lax.all_to_all(spatial, "seq", split_axis=2, concat_axis=1, tiled=True),
    )
    frame_all = jnp.arange(frames, dtype=jnp.int32)
    patch_ids = shard_idx * patches_dev + jnp.arange(patches_dev, dtype=jnp.int32)
    shaped_tm = (frames, patches_dev, heads, HD)
    queries_tm = query_pt[0].reshape(shaped_tm)
    keys_tm = key_pt[0].reshape(shaped_tm)
    values_tm = spatial_pt[0].reshape(shaped_tm)
    scores_tm = (
        jnp.einsum("fphd,gphd->phfg", queries_tm, keys_tm, preferred_element_type=jnp.float32)
        * scale
    )
    scores_tm = jnp.where(frame_all[None, None, None, :] < own_shape[0], scores_tm, NEG)
    weights_tm = softmax_rows(scores_tm).astype(jnp.bfloat16)
    temporal = jnp.einsum(
        "phfg,gphd->fphd", weights_tm, values_tm, preferred_element_type=jnp.float32
    )
    valid_tm = (frame_all[:, None] < own_shape[0]) & (patch_ids[None, :] < own_shape[1])
    temporal = jnp.where(valid_tm[:, :, None, None], temporal, 0.0).astype(jnp.bfloat16)
    temporal = temporal.reshape(1, frames, patches_dev, width)
    result = lax.all_to_all(temporal, "seq", split_axis=1, concat_axis=2, tiled=True)
    for section in range(sections):
        other = swapped(result, "grp", section)
        result = jnp.where(section_cross(route, group_idx, section), other, result)
    return result


def softmax_weights(scores):
    top = jnp.max(scores, axis=-1, keepdims=True)
    expo = jnp.exp(scores - top)
    return (expo * (1.0 / jnp.sum(expo, axis=-1, keepdims=True))).astype(jnp.bfloat16)


def nt_dot(a, b):
    return lax.dot_general(a, b, (((1,), (1,)), ((), ())), preferred_element_type=jnp.float32)


def kernel(
    plan, slot_ref, slot_f, out_tab, meta,
    q_hbm, k_hbm, v_hbm, qt_hbm, kt_hbm, o_ref,
    inp, xs, xr0, xr1, xr2, zs16, zq16, zs8, zq8, zs4, zq4, wts, bias, oz16, oz8, oz4, zr, xso, xro,
    in_sem, xss, xrs, xls, zss, zrs, zls,
):
    K16, K8, K4 = plan
    off8, off4 = 16 * K16, 16 * K16 + 8 * K8
    total = off4 + 4 * K4
    c = lax.axis_index("grp")
    z = lax.axis_index("seq")
    core = lax.rem(c, 2)
    xr = (xr0, xr1, xr2)
    barrier = pltpu.get_barrier_semaphore()

    def greet_x(d, _):
        pl.semaphore_signal(barrier, inc=1, device_id={"grp": lax.rem(c + d, 32)}, device_id_type=MESH)
        return 0

    def greet_z(d, _):
        pl.semaphore_signal(barrier, inc=1, device_id={"seq": lax.rem(z + d, 16)}, device_id_type=MESH)
        return 0

    lax.fori_loop(1, 16, greet_z, 0)
    lax.fori_loop(1, 32, greet_x, 0)

    loads = [
        pltpu.make_async_copy(ref.at[0, 0], inp.at[i], in_sem.at[i])
        for i, ref in enumerate((kt_hbm, qt_hbm, q_hbm, k_hbm, v_hbm))
    ]
    for load in loads:
        load.start()

    def pack(a):
        def group(s, _):
            for hg in range(4):
                for t in range(12):
                    b, m = divmod(t, 3)
                    rows = pl.ds(pl.multiple_of(64 * b + 16 * s, 16), 16)
                    lanes = pl.ds((3 * hg + m) * HD, HD)
                    dev = 2 * (4 * s + hg) + lax.rem(t + core, 2)
                    xs[a, dev, t // 2] = inp[a, rows, lanes]
            return 0

        lax.fori_loop(0, 4, group, 0)

    for a in range(2):
        loads[a].wait()
        pack(a)

    row_id = lax.broadcasted_iota(jnp.int32, (256, 256), 0)
    col_id = lax.broadcasted_iota(jnp.int32, (256, 256), 1)
    for i in range(3):
        period = 16 * 2**i
        same = (row_id & (period - 1)) == (col_id & (period - 1))
        bias[i] = jnp.where(same, 0.0, NEG)
    zr[total] = jnp.zeros((TILE, HD), jnp.bfloat16)

    for i in (2, 3, 4):
        loads[i].wait()
    scale = HD ** (-0.5)
    lane_id = lax.broadcasted_iota(jnp.int32, (1, 256), 1)
    key_bias = jnp.where(lane_id < meta[0], 0.0, NEG)

    def heads(hg, _):
        for m in range(3):
            lanes = pl.ds(pl.multiple_of((3 * hg + m) * HD, HD), HD)
            scores = nt_dot(inp[2, :, lanes], inp[3, :, lanes]) * scale + key_bias
            weights = softmax_weights(scores)
            out = jnp.dot(weights, inp[4, :, lanes], preferred_element_type=jnp.float32)
            out = out.astype(jnp.bfloat16)
            for b in range(4):
                t = 3 * b + m
                for s in range(4):
                    dev = 2 * (4 * s + hg) + lax.rem(t + core, 2)
                    xs[2, dev, t // 2] = out[64 * b + 16 * s : 64 * b + 16 * s + 16]
        return 0

    lax.fori_loop(0, 4, heads, 0)

    pl.semaphore_wait(barrier, 46)

    def x_send(src, dst, i):
        def one(d, _):
            dev = lax.rem(c + d, 32)
            pltpu.make_async_remote_copy(
                src_ref=src.at[dev], dst_ref=dst.at[c], send_sem=xss.at[i], recv_sem=xrs.at[i],
                device_id={"grp": dev}, device_id_type=MESH,
            ).start()
            return 0

        lax.fori_loop(1, 32, one, 0)
        pltpu.make_async_copy(src.at[c], dst.at[c], xls.at[i]).start()

    def x_wait(src, dst, i):
        part = dst.at[pl.ds(0, 31)]
        pltpu.make_async_copy(part, part, xrs.at[i]).wait()
        pltpu.make_async_copy(src.at[c], dst.at[c], xls.at[i]).wait()

    def x_drain(src, i):
        part = src.at[pl.ds(0, 31)]
        pltpu.make_async_copy(part, part, xss.at[i]).wait()

    for a in range(3):
        x_send(xs.at[a], xr[a], a)

    rings = ((16, zs16, zq16, 0), (8, zs8, zq8, off8), (4, zs4, zq4, off4))
    rings = tuple(r for r, k in zip(rings, plan) if k)
    slots = {16: K16, 8: K8, 4: K4}
    kind = {16: 0, 8: 1, 4: 2}

    def on_ring(size, run):
        if size == 16:
            run()
        else:
            pl.when(z < size)(run)

    def z_send(a, size, send, land, off):
        k_n = slots[size]
        i = 3 * a + kind[size]

        def fill(dev):
            for k in range(k_n):
                index = slot_ref[off + dev * k_n + k]
                send[a, dev, k] = xr[a][index // 6, lax.rem(index, 6)]

        def one(d, _):
            dev = lax.rem(z + d, size)
            fill(dev)
            pltpu.make_async_remote_copy(
                src_ref=send.at[a, dev], dst_ref=land.at[a, z], send_sem=zss.at[i], recv_sem=zrs.at[i],
                device_id={"seq": dev}, device_id_type=MESH,
            ).start()
            return 0

        lax.fori_loop(1, size, one, 0)
        fill(z)
        pltpu.make_async_copy(send.at[a, z], land.at[a, z], zls.at[i]).start()

    def z_wait(a, size, send, land):
        i = 3 * a + kind[size]
        part = land.at[a, pl.ds(0, size - 1)]
        pltpu.make_async_copy(part, part, zrs.at[i]).wait()
        pltpu.make_async_copy(send.at[a, z], land.at[a, z], zls.at[i]).wait()
        pltpu.make_async_copy(part, part, zss.at[i]).wait()

    for a in range(3):
        x_wait(xs.at[a], xr[a], a)
        for size, send, land, off in rings:
            on_ring(size, functools.partial(z_send, a, size, send, land, off))

    blocks = []
    for size, _, _, _ in rings:
        step = 16 // size
        for k in range(0, slots[size], step):
            blocks.append((size, k, min(step, slots[size] - k), len(blocks)))

    def block(land, a, size, k, n):
        if n == 1:
            return land[a, :, k].reshape(size * TILE, HD)
        return land[a, :, k : k + n].reshape(size * n * TILE, HD)

    def z_weights(size, land, off):
        for bsize, k, n, place in blocks:
            if bsize != size:
                continue
            rows = size * n * TILE
            scores = nt_dot(block(land, 1, size, k, n), block(land, 0, size, k, n)) * scale
            which = {1: 0, 2: 1, 4: 2}.get(n)
            if which is None:
                r = lax.broadcasted_iota(jnp.int32, (rows, rows), 0)
                q = lax.broadcasted_iota(jnp.int32, (rows, rows), 1)
                scores = jnp.where(lax.rem(r, n * TILE) == lax.rem(q, n * TILE), scores, NEG)
            else:
                scores = scores + bias[which, :rows, :rows]
            if size != 4:
                lane = lax.broadcasted_iota(jnp.int32, (1, rows), 1)
                frame = lane // (n * TILE)
                count = slot_f[off + z * slots[size] + k]
                if n == 2:
                    second = slot_f[off + z * slots[size] + k + 1]
                    count = jnp.where((lane // TILE) % 2 == 0, count, second)
                scores = scores + jnp.where(frame < count, 0.0, NEG)
            wts[place, :rows, :rows] = softmax_weights(scores)

    def z_values(size, land, back):
        for bsize, k, n, place in blocks:
            if bsize != size:
                continue
            rows = size * n * TILE
            out = jnp.dot(
                wts[place, :rows, :rows], block(land, 2, size, k, n), preferred_element_type=jnp.float32
            ).astype(jnp.bfloat16)
            out = out.reshape(size, n, TILE, HD)
            for j in range(n):
                back[:, k + j] = out[:, j]

    for a in range(2):
        for size, send, land, off in rings:
            on_ring(size, functools.partial(z_wait, a, size, send, land))
    for size, send, land, off in rings:
        on_ring(size, functools.partial(z_weights, size, land, off))

    backs = {16: oz16, 8: oz8, 4: oz4}

    def z_return(size, back, off):
        k_n = slots[size]
        i = 9 + kind[size]

        def one(d, _):
            dev = lax.rem(z + d, size)
            pltpu.make_async_remote_copy(
                src_ref=back.at[dev], dst_ref=zr.at[pl.ds(off + z * k_n, k_n)],
                send_sem=zss.at[i], recv_sem=zrs.at[i], device_id={"seq": dev}, device_id_type=MESH,
            ).start()
            return 0

        lax.fori_loop(1, size, one, 0)
        pltpu.make_async_copy(back.at[z], zr.at[pl.ds(off + z * k_n, k_n)], zls.at[i]).start()

    def z_return_wait(size, back, off):
        k_n = slots[size]
        i = 9 + kind[size]
        part = zr.at[pl.ds(off, (size - 1) * k_n)]
        pltpu.make_async_copy(part, part, zrs.at[i]).wait()
        pltpu.make_async_copy(back.at[z], zr.at[pl.ds(off + z * k_n, k_n)], zls.at[i]).wait()
        pltpu.make_async_copy(part, part, zss.at[i]).wait()

    def finish(size, send, land, off):
        z_wait(2, size, send, land)
        z_values(size, land, backs[size])
        z_return(size, backs[size], off)

    for size, send, land, off in rings:
        on_ring(size, functools.partial(finish, size, send, land, off))
    for size, send, land, off in rings:
        on_ring(size, functools.partial(z_return_wait, size, backs[size], off))

    def collect(dev, _):
        for i in range(6):
            xso[dev, i] = zr[out_tab[dev * 6 + i]]
        return 0

    lax.fori_loop(0, 32, collect, 0)
    x_send(xso, xro, 3)
    x_wait(xso, xro, 3)
    swap = meta[1]

    def place_out(s, _):
        for hg in range(4):
            for t in range(12):
                b, m = divmod(t, 3)
                rows = pl.ds(pl.multiple_of(64 * b + 16 * s, 16), 16)
                dev = 2 * (4 * s + hg) + lax.rem(t + swap, 2)
                o_ref[0, 0, rows, (3 * hg + m) * HD : (3 * hg + m + 1) * HD] = xro[dev, t // 2]
        return 0

    lax.fori_loop(0, 4, place_out, 0)
    for a in range(3):
        x_drain(xs.at[a], a)
    x_drain(xso, 3)


def packed(cid, plan, tables, arrays):
    K16, K8, K4 = plan
    total = 16 * K16 + 8 * K8 + 4 * K4
    bf = jnp.bfloat16
    n_blocks = K16 + (K8 + 1) // 2 + (K4 + 3) // 4
    smem = pl.BlockSpec(memory_space=pltpu.SMEM)
    k16, k8, k4 = max(K16, 1), max(K8, 1), max(K4, 1)
    return pl.pallas_call(
        functools.partial(kernel, plan),
        out_shape=jax.ShapeDtypeStruct(arrays[0].shape, bf),
        in_specs=[smem] * 4 + [pl.BlockSpec(memory_space=pl.ANY)] * 5,
        out_specs=pl.BlockSpec(memory_space=pltpu.VMEM),
        scratch_shapes=[
            pltpu.VMEM((5, 256, 12 * HD), bf),
            pltpu.VMEM((3, 32, 6, TILE, HD), bf),
            pltpu.VMEM((32, 6, TILE, HD), bf),
            pltpu.VMEM((32, 6, TILE, HD), bf),
            pltpu.VMEM((32, 6, TILE, HD), bf),
            pltpu.VMEM((3, 16, k16, TILE, HD), bf),
            pltpu.VMEM((3, 16, k16, TILE, HD), bf),
            pltpu.VMEM((3, 8, k8, TILE, HD), bf),
            pltpu.VMEM((3, 8, k8, TILE, HD), bf),
            pltpu.VMEM((3, 4, k4, TILE, HD), bf),
            pltpu.VMEM((3, 4, k4, TILE, HD), bf),
            pltpu.VMEM((n_blocks, 256, 256), bf),
            pltpu.VMEM((3, 256, 256), jnp.float32),
            pltpu.VMEM((16, k16, TILE, HD), bf),
            pltpu.VMEM((8, k8, TILE, HD), bf),
            pltpu.VMEM((4, k4, TILE, HD), bf),
            pltpu.VMEM((total + 1, TILE, HD), bf),
            pltpu.VMEM((32, 6, TILE, HD), bf),
            pltpu.VMEM((32, 6, TILE, HD), bf),
            pltpu.SemaphoreType.DMA((5,)),
            pltpu.SemaphoreType.DMA((4,)),
            pltpu.SemaphoreType.DMA((4,)),
            pltpu.SemaphoreType.DMA((4,)),
            pltpu.SemaphoreType.DMA((12,)),
            pltpu.SemaphoreType.DMA((12,)),
            pltpu.SemaphoreType.DMA((12,)),
        ],
        compiler_params=pltpu.CompilerParams(
            collective_id=cid, has_side_effects=True, vmem_limit_bytes=48 * 1024 * 1024
        ),
    )(*tables, *arrays)


def units_of(clip_shape, core):
    frames, blocks = clip_shape[:, 0], clip_shape[:, 1] // 64
    clips = jnp.arange(32, dtype=jnp.int32)
    count = (3 * blocks + 1 - ((core + clips) & 1)) // 2
    before = (frames[None, :] > frames[:, None]) | (
        (frames[None, :] == frames[:, None]) & (clips[None, :] < clips[:, None])
    )
    return count, jnp.sum(jnp.where(before, count[None, :], 0), axis=1)


def needs(clip_shape):
    frames, blocks = clip_shape[:, 0], clip_shape[:, 1] // 64
    clips = jnp.arange(32, dtype=jnp.int32)
    worst = []
    for least in (16, 8, 4):
        per_core = [
            jnp.sum(jnp.where(frames >= least, (3 * blocks + 1 - ((core + clips) & 1)) // 2, 0))
            for core in range(2)
        ]
        worst.append(jnp.maximum(*per_core))
    return worst


def trace_anchor(route):
    clips = jnp.arange(32, dtype=jnp.int32)
    anchor = clips
    for section in range(5):
        width = 1 << section
        low = route.reshape(-1, 2, width)[:, :1]
        cross = (jnp.right_shift(low, section) & 1) == 1
        halves = anchor.reshape(-1, 2, width)
        anchor = jnp.where(cross, halves[:, ::-1], halves).reshape(32)
    return anchor


def tables_of(plan, clip_shape, route):
    K16, K8, K4 = plan
    off8, off4 = 16 * K16, 16 * K16 + 8 * K8
    total = off4 + 4 * K4
    group, frame = lax.axis_index("grp"), lax.axis_index("seq")
    count, start = units_of(clip_shape, group & 1)
    place = np.zeros(total, np.int32)
    own = np.zeros(total, np.int32)
    for off, size, k_n in ((0, 16, K16), (off8, 8, K8), (off4, 4, K4)):
        for j in range(size):
            for k in range(k_n):
                place[off + j * k_n + k] = off + k * size + j
                own[off + j * k_n + k] = size
    inside = jnp.asarray(place)[:, None] - start[None, :]
    hit = (inside >= 0) & (inside < count[None, :])
    clips = jnp.arange(32, dtype=jnp.int32)
    slot = jnp.sum(jnp.where(hit, clips[None, :] * 6 + inside, 0), axis=1)
    slot_f = jnp.sum(jnp.where(hit, clip_shape[:, 0][None, :], 0), axis=1)
    slot_f = jnp.where(slot_f == 0, jnp.asarray(own), slot_f)
    anchor = trace_anchor(route)
    chosen = anchor[:, None] == clips[None, :]

    def pick(values):
        return jnp.sum(jnp.where(chosen, values[None, :], 0), axis=1)

    first, units, frames = pick(start), pick(count), pick(clip_shape[:, 0])
    t = jnp.arange(6, dtype=jnp.int32)[None, :]
    unit = first[:, None] + t
    spot = jnp.full(unit.shape, total, jnp.int32)
    for off, size, k_n in ((0, 16, K16), (off8, 8, K8), (off4, 4, K4)):
        if k_n:
            inner = unit - off
            here = (inner >= 0) & (inner < size * k_n)
            spot = jnp.where(here, off + (inner % size) * k_n + inner // size, spot)
    good = (t < units[:, None]) & (frame < frames[:, None])
    out_tab = jnp.where(good, spot, total).reshape(-1)
    mine = clips == group
    own_patches = jnp.sum(jnp.where(mine, clip_shape[:, 1], 0))
    own_swap = jnp.sum(jnp.where(mine, anchor, 0)) & 1
    meta = jnp.stack([own_patches, own_swap]).astype(jnp.int32)
    return slot.astype(jnp.int32), slot_f.astype(jnp.int32), out_tab.astype(jnp.int32), meta


def body(query_sp, key_sp, value_sp, query_tm, key_tm, clip_shape, route):
    n16, n8, n4 = needs(clip_shape)
    fits = []
    for K16, K8, K4 in PLANS:
        a, b, d = 16 * K16, 16 * K16 + 8 * K8, 16 * K16 + 8 * K8 + 4 * K4
        fits.append((n16 <= a) & (n8 <= b) & (n4 <= d))
    choice = jnp.int32(len(PLANS))
    for i in reversed(range(len(PLANS))):
        choice = jnp.where(fits[i], i, choice)

    def run(i, *args):
        arrays, (shape, way) = args[:5], args[5:]
        return packed(i, PLANS[i], tables_of(PLANS[i], shape, way), arrays)

    branches = [functools.partial(run, i) for i in range(len(PLANS))] + [general]
    return lax.switch(
        choice, branches, query_sp, key_sp, value_sp, query_tm, key_tm, clip_shape, route
    )


def solution(mesh):
    in_specs = (
        P("grp", "seq", None, None),
        P("grp", "seq", None, None),
        P("grp", "seq", None, None),
        P("grp", "seq", None, None),
        P("grp", "seq", None, None),
        P(),
        P(),
    )
    out_specs = P("grp", "seq", None, None)
    return jax.shard_map(body, mesh=mesh, in_specs=in_specs, out_specs=out_specs, check_vma=False)
```

```python
import functools

import jax
import jax.numpy as jnp
from jax import lax
from jax.experimental import pallas as pl
from jax.experimental.pallas import tpu as pltpu
from jax.sharding import PartitionSpec as P

HD = 128
TILE = 16
MESH = pl.DeviceIdType.MESH
NEG = -1e30
PLANS = (
    ((6, 11, 5), (3, 2, 17), (1, 2, 21)),
    ((6, 12, 6), (3, 2, 19), (2, 1, 34)),
    ((4, 13, 7), (2, 2, 18), (1, 1, 23)),
)


def capacity(plan):
    sums = []
    for _, count, slots in plan:
        sums.append(count * slots + (sums[-1] if sums else 0))
    return sums


def swapped(value, axis, bit):
    mask = 2**bit
    pairs = [(source, source ^ mask) for source in range(lax.axis_size(axis))]
    return lax.ppermute(value, axis, pairs)


def softmax_rows(scores):
    top = jnp.max(scores, axis=-1, keepdims=True)
    expo = jnp.exp(scores - top)
    return expo / jnp.sum(expo, axis=-1, keepdims=True)


def section_cross(route, group_idx, section):
    partner = jnp.bitwise_xor(group_idx, 1 << section)
    lower = jnp.minimum(group_idx, partner)
    return jnp.bitwise_and(jnp.right_shift(route[lower], section), 1) == 1


def general(query_sp, key_sp, value_sp, query_tm, key_tm, clip_shape, route):
    groups = lax.axis_size("grp")
    shards = lax.axis_size("seq")
    group_idx = lax.axis_index("grp")
    shard_idx = lax.axis_index("seq")
    sections = groups.bit_length() - 1
    frames_dev = query_sp.shape[1]
    patches = query_sp.shape[2]
    width = query_sp.shape[3]
    heads = width // HD
    frames = frames_dev * shards
    patches_dev = patches // shards
    scale = HD ** (-0.5)
    own_shape = clip_shape[group_idx]
    frame_ids = shard_idx * frames_dev + jnp.arange(frames_dev, dtype=jnp.int32)
    patch_all = jnp.arange(patches, dtype=jnp.int32)
    shaped = (frames_dev, patches, heads, HD)
    queries = query_sp[0].reshape(shaped)
    keys = key_sp[0].reshape(shaped)
    values = value_sp[0].reshape(shaped)
    scores = (
        jnp.einsum("fphd,fqhd->fhpq", queries, keys, preferred_element_type=jnp.float32) * scale
    )
    scores = jnp.where(patch_all[None, None, None, :] < own_shape[1], scores, NEG)
    weights = softmax_rows(scores).astype(jnp.bfloat16)
    spatial = jnp.einsum("fhpq,fqhd->fphd", weights, values, preferred_element_type=jnp.float32)
    valid_sp = (frame_ids[:, None] < own_shape[0]) & (patch_all[None, :] < own_shape[1])
    spatial = jnp.where(valid_sp[:, :, None, None], spatial, 0.0).astype(jnp.bfloat16)
    spatial = spatial.reshape(1, frames_dev, patches, width)
    query_pt, key_pt, spatial_pt = (
        lax.all_to_all(query_tm, "seq", split_axis=2, concat_axis=1, tiled=True),
        lax.all_to_all(key_tm, "seq", split_axis=2, concat_axis=1, tiled=True),
        lax.all_to_all(spatial, "seq", split_axis=2, concat_axis=1, tiled=True),
    )
    frame_all = jnp.arange(frames, dtype=jnp.int32)
    patch_ids = shard_idx * patches_dev + jnp.arange(patches_dev, dtype=jnp.int32)
    shaped_tm = (frames, patches_dev, heads, HD)
    queries_tm = query_pt[0].reshape(shaped_tm)
    keys_tm = key_pt[0].reshape(shaped_tm)
    values_tm = spatial_pt[0].reshape(shaped_tm)
    scores_tm = (
        jnp.einsum("fphd,gphd->phfg", queries_tm, keys_tm, preferred_element_type=jnp.float32)
        * scale
    )
    scores_tm = jnp.where(frame_all[None, None, None, :] < own_shape[0], scores_tm, NEG)
    weights_tm = softmax_rows(scores_tm).astype(jnp.bfloat16)
    temporal = jnp.einsum(
        "phfg,gphd->fphd", weights_tm, values_tm, preferred_element_type=jnp.float32
    )
    valid_tm = (frame_all[:, None] < own_shape[0]) & (patch_ids[None, :] < own_shape[1])
    temporal = jnp.where(valid_tm[:, :, None, None], temporal, 0.0).astype(jnp.bfloat16)
    temporal = temporal.reshape(1, frames, patches_dev, width)
    result = lax.all_to_all(temporal, "seq", split_axis=1, concat_axis=2, tiled=True)
    for section in range(sections):
        other = swapped(result, "grp", section)
        result = jnp.where(section_cross(route, group_idx, section), other, result)
    return result


def softmax_weights(scores):
    top = jnp.max(scores, axis=-1, keepdims=True)
    expo = jnp.exp(scores - top)
    return (expo * (1.0 / jnp.sum(expo, axis=-1, keepdims=True))).astype(jnp.bfloat16)


def nt_dot(a, b):
    return lax.dot_general(a, b, (((1,), (1,)), ((), ())), preferred_element_type=jnp.float32)


def kernel(
    plan, shape_ref, route_ref,
    q_hbm, k_hbm, v_hbm, qt_hbm, kt_hbm, o_ref,
    inp, xs, xr0, xr1, xr2, zs16, zq16, oz16, zs8, zq8, oz8, zs4, zq4, oz4, wts, bias, zr, xso, xro,
    table, slot_ref, first, units, out_tab,
    in_sem, xss, xrs, xls, zss, zrs, zls, tab_sem,
):
    total = capacity(plan)[-1]
    c = lax.axis_index("grp")
    z = lax.axis_index("seq")
    core = lax.rem(c, 2)
    xr = (xr0, xr1, xr2)
    barrier = pltpu.get_barrier_semaphore()

    def greet_x(d, _):
        pl.semaphore_signal(barrier, inc=1, device_id={"grp": lax.rem(c + d, 32)}, device_id_type=MESH)
        return 0

    def greet_z(d, _):
        pl.semaphore_signal(barrier, inc=1, device_id={"seq": lax.rem(z + d, 16)}, device_id_type=MESH)
        return 0

    lax.fori_loop(1, 16, greet_z, 0)
    lax.fori_loop(1, 32, greet_x, 0)

    loads = [
        pltpu.make_async_copy(ref.at[0, 0], inp.at[i], in_sem.at[i])
        for i, ref in enumerate((kt_hbm, qt_hbm, q_hbm, k_hbm, v_hbm))
    ]
    for load in loads:
        load.start()

    def pack(a):
        def group(s, _):
            for hg in range(4):
                for t in range(12):
                    b, m = divmod(t, 3)
                    rows = pl.ds(pl.multiple_of(64 * b + 16 * s, 16), 16)
                    lanes = pl.ds((3 * hg + m) * HD, HD)
                    dev = 2 * (4 * s + hg) + lax.rem(t + core, 2)
                    xs[a, dev, t // 2] = inp[a, rows, lanes]
            return 0

        lax.fori_loop(0, 4, group, 0)

    def x_send(src, dst, i):
        def one(d, _):
            other = d >= 15
            e = jnp.where(other, d - 15, jnp.where(d >= 10, d + 1, d))
            row, col = lax.rem(e // 4 + 2 + c // 8, 4), lax.rem(lax.rem(e, 4) + 2 + lax.rem(c // 2, 4), 4)
            dev = 8 * row + 2 * col + lax.rem(core + jnp.where(other, 1, 0), 2)
            pltpu.make_async_remote_copy(
                src_ref=src.at[dev], dst_ref=dst.at[c], send_sem=xss.at[i], recv_sem=xrs.at[i],
                device_id={"grp": dev}, device_id_type=MESH,
            ).start()
            return 0

        lax.fori_loop(0, 31, one, 0)
        pltpu.make_async_copy(src.at[c], dst.at[c], xls.at[i]).start()

    def x_wait(src, dst, i):
        part = dst.at[pl.ds(0, 31)]
        pltpu.make_async_copy(part, part, xrs.at[i]).wait()
        pltpu.make_async_copy(src.at[c], dst.at[c], xls.at[i]).wait()

    def x_drain(src, i):
        part = src.at[pl.ds(0, 31)]
        pltpu.make_async_copy(part, part, xss.at[i]).wait()

    loads[0].wait()
    pack(0)
    pl.semaphore_wait(barrier, 46)
    x_send(xs.at[0], xr[0], 0)
    loads[1].wait()
    pack(1)
    x_send(xs.at[1], xr[1], 1)

    def count_units(clip, sums):
        frames = shape_ref[0, clip]
        count = (3 * (shape_ref[1, clip] >> 6) + 1 - ((core + clip) & 1)) >> 1
        units[clip] = count
        is16, is8 = frames == 16, frames == 8
        first[clip] = jnp.where(is16, sums[0], jnp.where(is8, sums[1], sums[2]))
        return (
            sums[0] + jnp.where(is16, count, 0),
            sums[1] + jnp.where(is8, count, 0),
            sums[2] + jnp.where(is16 | is8, 0, count),
        )

    zero = jnp.int32(0)
    n16, n8, _ = lax.fori_loop(0, 32, count_units, (zero, zero, zero))

    row = lax.broadcasted_iota(jnp.int32, table.shape[1:], 0)
    lane = lax.broadcasted_iota(jnp.int32, table.shape[1:], 1)
    place = 128 * row + lane

    def find_slots(clip, found):
        unit, count = found
        frames = shape_ref[0, clip]
        start = first[clip] + jnp.where(frames == 16, 0, jnp.where(frames == 8, n16, n16 + n8))
        first[clip] = start
        inner = place - start
        hit = (inner >= 0) & (inner < units[clip])
        return jnp.where(hit, inner + 6 * clip, unit), jnp.where(hit, frames, count)

    unit, count = lax.fori_loop(0, 32, find_slots, (jnp.zeros_like(place), jnp.full_like(place, 16)))
    table[0] = unit
    table[1] = count
    to_smem = pltpu.make_async_copy(table, slot_ref, tab_sem.at[0])
    to_smem.start()

    row_id = lax.broadcasted_iota(jnp.int32, (256, 256), 0)
    col_id = lax.broadcasted_iota(jnp.int32, (256, 256), 1)
    for i in range(3):
        period = 16 * 2**i
        same = (row_id & (period - 1)) == (col_id & (period - 1))
        bias[i] = jnp.where(same, 0.0, NEG)
    zr[total] = jnp.zeros((TILE, HD), jnp.bfloat16)

    for i in (2, 3, 4):
        loads[i].wait()
    scale = HD ** (-0.5)
    lane_id = lax.broadcasted_iota(jnp.int32, (1, 256), 1)
    key_bias = jnp.where(lane_id < shape_ref[1, c], 0.0, NEG)

    def heads(hg, _):
        for m in range(3):
            lanes = pl.ds(pl.multiple_of((3 * hg + m) * HD, HD), HD)
            scores = nt_dot(inp[2, :, lanes], inp[3, :, lanes]) * scale + key_bias
            weights = softmax_weights(scores)
            out = jnp.dot(weights, inp[4, :, lanes], preferred_element_type=jnp.float32)
            out = out.astype(jnp.bfloat16)
            for b in range(4):
                t = 3 * b + m
                for s in range(4):
                    dev = 2 * (4 * s + hg) + lax.rem(t + core, 2)
                    xs[2, dev, t // 2] = out[64 * b + 16 * s : 64 * b + 16 * s + 16]
        return 0

    lax.fori_loop(0, 4, heads, 0)
    x_send(xs.at[2], xr[2], 2)
    to_smem.wait()

    class Ring:
        def __init__(self, kind, sources, send, land, back):
            self.kind, self.sources, self.send, self.land, self.back = kind, sources, send, land, back
            self.start, self.count, self.slots = plan[kind]
            self.off = capacity(plan)[kind] - self.count * self.slots
            self.place = lax.rem(z - self.start + 16, 16)
            self.works = self.place < self.count

    rings = (Ring(0, 16, zs16, zq16, oz16), Ring(1, 8, zs8, zq8, oz8), Ring(2, 4, zs4, zq4, oz4))

    def entry(kind, r):
        return slot_ref[kind, r >> 7, r & 127]

    def on_sources(ring, run):
        if ring.sources == 16:
            run()
        else:
            pl.when(z < ring.sources)(run)

    def z_send(a, ring):
        i = 3 * a + ring.kind

        def one(d, _):
            j = lax.rem(z + d, ring.count)
            dev = lax.rem(ring.start + j, 16)
            for k in range(ring.slots):
                index = entry(0, ring.off + j * ring.slots + k)
                ring.send[a, j, k] = xr[a][index // 6, lax.rem(index, 6)]

            @pl.when(dev != z)
            def _():
                pltpu.make_async_remote_copy(
                    src_ref=ring.send.at[a, j], dst_ref=ring.land.at[a, z], send_sem=zss.at[i], recv_sem=zrs.at[i],
                    device_id={"seq": dev}, device_id_type=MESH,
                ).start()

            @pl.when(dev == z)
            def _():
                pltpu.make_async_copy(ring.send.at[a, j], ring.land.at[a, z], zls.at[i]).start()

            return 0

        lax.fori_loop(0, ring.count, one, 0)

    def z_sent(a, ring):
        i = 3 * a + ring.kind
        for mine in (0, 1):
            if ring.count > mine:

                @pl.when(ring.works if mine else jnp.logical_not(ring.works))
                def _():
                    part = ring.send.at[a, pl.ds(0, ring.count - mine)]
                    pltpu.make_async_copy(part, part, zss.at[i]).wait()

    def z_wait(a, ring):
        i = 3 * a + ring.kind
        part = ring.land.at[a, pl.ds(0, ring.sources - 1)]
        pltpu.make_async_copy(part, part, zrs.at[i]).wait()
        one = ring.land.at[a, 0]
        pltpu.make_async_copy(one, one, zls.at[i]).wait()

    for a in range(3):
        x_wait(xs.at[a], xr[a], a)
        for ring in rings:
            on_sources(ring, functools.partial(z_send, a, ring))

    def trace(group):
        for b in reversed(range(5)):
            low = group & (31 - (1 << b))
            group = group ^ (((route_ref[low] >> b) & 1) << b)
        return group

    def route_units(group, _):
        clip = trace(group)
        start = first[clip]
        count = jnp.where(z < shape_ref[0, clip], units[clip], 0)
        for i in range(6):
            out_tab[group * 6 + i] = jnp.where(i < count, start + i, total)
        return 0

    lax.fori_loop(0, 32, route_units, 0)

    for ring in rings:
        step = 16 // ring.sources
        ring.blocks = [(k, min(step, ring.slots - k), k // step) for k in range(0, ring.slots, step)]

    def block(ring, a, k, n):
        return ring.land[a, :, k : k + n].reshape(ring.sources * n * TILE, HD)

    def z_weights(ring):
        for a in range(2):
            z_wait(a, ring)
        for k, n, at in ring.blocks:
            rows = ring.sources * n * TILE
            scores = nt_dot(block(ring, 1, k, n), block(ring, 0, k, n)) * scale
            which = {1: 0, 2: 1, 4: 2}.get(n)
            if which is None:
                r = lax.broadcasted_iota(jnp.int32, (rows, rows), 0)
                q = lax.broadcasted_iota(jnp.int32, (rows, rows), 1)
                scores = jnp.where(lax.rem(r, n * TILE) == lax.rem(q, n * TILE), scores, NEG)
            else:
                scores = scores + bias[which, :rows, :rows]
            if ring.kind < 2:
                lane = lax.broadcasted_iota(jnp.int32, (1, rows), 1)
                frame = lane // (n * TILE)
                spot = ring.off + ring.place * ring.slots + k
                count = entry(1, spot)
                if n == 2:
                    count = jnp.where((lane // TILE) % 2 == 0, count, entry(1, spot + 1))
                scores = scores + jnp.where(frame < count, 0.0, NEG)
            wts[ring.kind, at, :rows, :rows] = softmax_weights(scores)

    def z_values(ring):
        z_wait(2, ring)
        for k, n, at in ring.blocks:
            rows = ring.sources * n * TILE
            out = jnp.dot(
                wts[ring.kind, at, :rows, :rows], block(ring, 2, k, n), preferred_element_type=jnp.float32
            ).astype(jnp.bfloat16)
            out = out.reshape(ring.sources, n, TILE, HD)
            for j in range(n):
                ring.back[:, k + j] = out[:, j]
        i = 9 + ring.kind
        home = zr.at[pl.ds(ring.off + ring.place * ring.slots, ring.slots)]

        def one(d, _):
            dev = lax.rem(z + d, ring.sources)
            pltpu.make_async_remote_copy(
                src_ref=ring.back.at[dev], dst_ref=home, send_sem=zss.at[i], recv_sem=zrs.at[i],
                device_id={"seq": dev}, device_id_type=MESH,
            ).start()
            return 0

        lax.fori_loop(1, ring.sources, one, 0)
        pltpu.make_async_copy(ring.back.at[z], home, zls.at[i]).start()

    def z_home(ring):
        i = 9 + ring.kind
        for mine in (0, 1):

            @pl.when(ring.works if mine else jnp.logical_not(ring.works))
            def _():
                if ring.count > mine:
                    part = zr.at[pl.ds(ring.off, (ring.count - mine) * ring.slots)]
                    pltpu.make_async_copy(part, part, zrs.at[i]).wait()
                if mine:
                    one = ring.back.at[0]
                    pltpu.make_async_copy(one, one, zls.at[i]).wait()

    def z_returned(ring):
        part = ring.back.at[pl.ds(0, ring.sources - 1)]
        pltpu.make_async_copy(part, part, zss.at[9 + ring.kind]).wait()

    for ring in rings:
        pl.when(ring.works)(functools.partial(z_weights, ring))
    for ring in rings:
        pl.when(ring.works)(functools.partial(z_values, ring))
    for ring in rings:
        on_sources(ring, functools.partial(z_home, ring))

    def collect(dev, _):
        for i in range(6):
            xso[dev, i] = zr[out_tab[dev * 6 + i]]
        return 0

    lax.fori_loop(0, 32, collect, 0)
    x_send(xso, xro, 3)
    x_wait(xso, xro, 3)
    swap = trace(c) & 1

    def place_out(s, _):
        for hg in range(4):
            for t in range(12):
                b, m = divmod(t, 3)
                rows = pl.ds(pl.multiple_of(64 * b + 16 * s, 16), 16)
                dev = 2 * (4 * s + hg) + lax.rem(t + swap, 2)
                o_ref[0, 0, rows, (3 * hg + m) * HD : (3 * hg + m + 1) * HD] = xro[dev, t // 2]
        return 0

    lax.fori_loop(0, 4, place_out, 0)
    for a in range(3):
        x_drain(xs.at[a], a)
    x_drain(xso, 3)
    for ring in rings:
        for a in range(3):
            on_sources(ring, functools.partial(z_sent, a, ring))
        pl.when(ring.works)(functools.partial(z_returned, ring))


def packed(cid, plan, clip_shape, route, arrays):
    total = capacity(plan)[-1]
    rows = (total + 1023) // 1024 * 8
    bf = jnp.bfloat16
    smem = pl.BlockSpec(memory_space=pltpu.SMEM)
    exchange = []
    for sources, (_, count, slots) in zip((16, 8, 4), plan):
        exchange.append(pltpu.VMEM((3, count, slots, TILE, HD), bf))
        exchange.append(pltpu.VMEM((3, sources, slots, TILE, HD), bf))
        exchange.append(pltpu.VMEM((sources, slots, TILE, HD), bf))
    n_blocks = max(-(-slots // (16 // sources)) for sources, (_, _, slots) in zip((16, 8, 4), plan))
    return pl.pallas_call(
        functools.partial(kernel, plan),
        out_shape=jax.ShapeDtypeStruct(arrays[0].shape, bf),
        in_specs=[smem] * 2 + [pl.BlockSpec(memory_space=pl.ANY)] * 5,
        out_specs=pl.BlockSpec(memory_space=pltpu.VMEM),
        scratch_shapes=[
            pltpu.VMEM((5, 256, 12 * HD), bf),
            pltpu.VMEM((3, 32, 6, TILE, HD), bf),
            pltpu.VMEM((32, 6, TILE, HD), bf),
            pltpu.VMEM((32, 6, TILE, HD), bf),
            pltpu.VMEM((32, 6, TILE, HD), bf),
            *exchange,
            pltpu.VMEM((3, n_blocks, 256, 256), bf),
            pltpu.VMEM((3, 256, 256), jnp.float32),
            pltpu.VMEM((total + 1, TILE, HD), bf),
            pltpu.VMEM((32, 6, TILE, HD), bf),
            pltpu.VMEM((32, 6, TILE, HD), bf),
            pltpu.VMEM((2, rows, 128), jnp.int32),
            pltpu.SMEM((2, rows, 128), jnp.int32),
            pltpu.SMEM((32,), jnp.int32),
            pltpu.SMEM((32,), jnp.int32),
            pltpu.SMEM((192,), jnp.int32),
            pltpu.SemaphoreType.DMA((5,)),
            pltpu.SemaphoreType.DMA((4,)),
            pltpu.SemaphoreType.DMA((4,)),
            pltpu.SemaphoreType.DMA((4,)),
            pltpu.SemaphoreType.DMA((12,)),
            pltpu.SemaphoreType.DMA((12,)),
            pltpu.SemaphoreType.DMA((12,)),
            pltpu.SemaphoreType.DMA((1,)),
        ],
        compiler_params=pltpu.CompilerParams(
            collective_id=cid, has_side_effects=True, vmem_limit_bytes=56 * 1024 * 1024
        ),
    )(clip_shape, route, *arrays)


def plan_of(clip_shape):
    frames, patches = clip_shape.T[:1], clip_shape.T[1:]
    kind = jnp.arange(6, dtype=jnp.int32)[:, None]
    clips = jnp.arange(32, dtype=jnp.int32)[None, :]
    units = (3 * (patches >> 6) + 1 - ((kind + clips) & 1)) >> 1
    needed = jnp.sum(jnp.where(frames >= (16 >> (kind >> 1)), units, 0), axis=1)
    over = 0
    for plan in PLANS:
        a, b, d = capacity(plan)
        at = jnp.arange(6, dtype=jnp.int32) >> 1
        held = jnp.where(at == 0, a, jnp.where(at == 1, b, d))
        over = over + (needed > held).astype(jnp.int32)
    return jnp.max(over)


def body(query_sp, key_sp, value_sp, query_tm, key_tm, clip_shape, route):
    choice = plan_of(clip_shape)

    def run(i, *args):
        arrays, (shape, way) = args[:5], args[5:]
        return packed(i, PLANS[i], shape.T, way, arrays)

    branches = [functools.partial(run, i) for i in range(len(PLANS))] + [general]
    return lax.switch(
        choice, branches, query_sp, key_sp, value_sp, query_tm, key_tm, clip_shape, route
    )


def solution(mesh):
    in_specs = (
        P("grp", "seq", None, None),
        P("grp", "seq", None, None),
        P("grp", "seq", None, None),
        P("grp", "seq", None, None),
        P("grp", "seq", None, None),
        P(),
        P(),
    )
    out_specs = P("grp", "seq", None, None)
    return jax.shard_map(body, mesh=mesh, in_specs=in_specs, out_specs=out_specs, check_vma=False)
```

```python
import functools

import jax
import jax.numpy as jnp
from jax import lax
from jax.experimental import pallas as pl
from jax.experimental.pallas import tpu as pltpu
from jax.sharding import PartitionSpec as P

HD = 128
TILE = 16
MESH = pl.DeviceIdType.MESH
NEG = -1e30
PLANS = (
    ((6, 12, 2), (3, 2, 10), (1, 2, 11)),
    ((6, 12, 3), (3, 2, 9), (2, 1, 18)),
    ((5, 14, 3), (3, 2, 11), (1, 2, 8)),
)


def capacity(plan):
    sums = []
    for _, count, slots in plan:
        sums.append(count * slots + (sums[-1] if sums else 0))
    return sums


def swapped(value, axis, bit):
    mask = 2**bit
    pairs = [(source, source ^ mask) for source in range(lax.axis_size(axis))]
    return lax.ppermute(value, axis, pairs)


def softmax_rows(scores):
    top = jnp.max(scores, axis=-1, keepdims=True)
    expo = jnp.exp(scores - top)
    return expo / jnp.sum(expo, axis=-1, keepdims=True)


def section_cross(route, group_idx, section):
    partner = jnp.bitwise_xor(group_idx, 1 << section)
    lower = jnp.minimum(group_idx, partner)
    return jnp.bitwise_and(jnp.right_shift(route[lower], section), 1) == 1


def general(query_sp, key_sp, value_sp, query_tm, key_tm, clip_shape, route):
    groups = lax.axis_size("grp")
    shards = lax.axis_size("seq")
    group_idx = lax.axis_index("grp")
    shard_idx = lax.axis_index("seq")
    sections = groups.bit_length() - 1
    frames_dev = query_sp.shape[1]
    patches = query_sp.shape[2]
    width = query_sp.shape[3]
    heads = width // HD
    frames = frames_dev * shards
    patches_dev = patches // shards
    scale = HD ** (-0.5)
    own_shape = clip_shape[group_idx]
    frame_ids = shard_idx * frames_dev + jnp.arange(frames_dev, dtype=jnp.int32)
    patch_all = jnp.arange(patches, dtype=jnp.int32)
    shaped = (frames_dev, patches, heads, HD)
    queries = query_sp[0].reshape(shaped)
    keys = key_sp[0].reshape(shaped)
    values = value_sp[0].reshape(shaped)
    scores = (
        jnp.einsum("fphd,fqhd->fhpq", queries, keys, preferred_element_type=jnp.float32) * scale
    )
    scores = jnp.where(patch_all[None, None, None, :] < own_shape[1], scores, NEG)
    weights = softmax_rows(scores).astype(jnp.bfloat16)
    spatial = jnp.einsum("fhpq,fqhd->fphd", weights, values, preferred_element_type=jnp.float32)
    valid_sp = (frame_ids[:, None] < own_shape[0]) & (patch_all[None, :] < own_shape[1])
    spatial = jnp.where(valid_sp[:, :, None, None], spatial, 0.0).astype(jnp.bfloat16)
    spatial = spatial.reshape(1, frames_dev, patches, width)
    query_pt, key_pt, spatial_pt = (
        lax.all_to_all(query_tm, "seq", split_axis=2, concat_axis=1, tiled=True),
        lax.all_to_all(key_tm, "seq", split_axis=2, concat_axis=1, tiled=True),
        lax.all_to_all(spatial, "seq", split_axis=2, concat_axis=1, tiled=True),
    )
    frame_all = jnp.arange(frames, dtype=jnp.int32)
    patch_ids = shard_idx * patches_dev + jnp.arange(patches_dev, dtype=jnp.int32)
    shaped_tm = (frames, patches_dev, heads, HD)
    queries_tm = query_pt[0].reshape(shaped_tm)
    keys_tm = key_pt[0].reshape(shaped_tm)
    values_tm = spatial_pt[0].reshape(shaped_tm)
    scores_tm = (
        jnp.einsum("fphd,gphd->phfg", queries_tm, keys_tm, preferred_element_type=jnp.float32)
        * scale
    )
    scores_tm = jnp.where(frame_all[None, None, None, :] < own_shape[0], scores_tm, NEG)
    weights_tm = softmax_rows(scores_tm).astype(jnp.bfloat16)
    temporal = jnp.einsum(
        "phfg,gphd->fphd", weights_tm, values_tm, preferred_element_type=jnp.float32
    )
    valid_tm = (frame_all[:, None] < own_shape[0]) & (patch_ids[None, :] < own_shape[1])
    temporal = jnp.where(valid_tm[:, :, None, None], temporal, 0.0).astype(jnp.bfloat16)
    temporal = temporal.reshape(1, frames, patches_dev, width)
    result = lax.all_to_all(temporal, "seq", split_axis=1, concat_axis=2, tiled=True)
    for section in range(sections):
        other = swapped(result, "grp", section)
        result = jnp.where(section_cross(route, group_idx, section), other, result)
    return result


def softmax_weights(scores):
    top = jnp.max(scores, axis=-1, keepdims=True)
    expo = jnp.exp(scores - top)
    return (expo * (1.0 / jnp.sum(expo, axis=-1, keepdims=True))).astype(jnp.bfloat16)


def nt_dot(a, b):
    return lax.dot_general(a, b, (((1,), (1,)), ((), ())), preferred_element_type=jnp.float32)


def kernel(
    plan, shape_ref, route_ref,
    q_hbm, k_hbm, v_hbm, qt_hbm, kt_hbm, o_ref,
    inp, xs, *refs,
):
    total = capacity(plan)[-1]
    xr, refs = (refs[0:3], refs[3:6]), refs[6:]
    exchange, refs = (refs[0:9], refs[9:18]), refs[18:]
    wts, bias, zr0, zr1, xso, xro, table, slot_ref, first, units, out_tab, *refs = refs
    in_sem, xss, xrs, xls, zss, zrs, zls, tab_sem = refs
    zr = (zr0, zr1)
    c = lax.axis_index("grp")
    z = lax.axis_index("seq")
    core = lax.rem(c, 2)
    barrier = pltpu.get_barrier_semaphore()

    def greet_x(d, _):
        pl.semaphore_signal(barrier, inc=1, device_id={"grp": lax.rem(c + d, 32)}, device_id_type=MESH)
        return 0

    def greet_z(d, _):
        pl.semaphore_signal(barrier, inc=1, device_id={"seq": lax.rem(z + d, 16)}, device_id_type=MESH)
        return 0

    lax.fori_loop(1, 16, greet_z, 0)
    lax.fori_loop(1, 32, greet_x, 0)

    loads = [
        pltpu.make_async_copy(ref.at[0, 0], inp.at[i], in_sem.at[i])
        for i, ref in enumerate((kt_hbm, qt_hbm, q_hbm, k_hbm, v_hbm))
    ]
    for load in loads:
        load.start()

    def half_of(i, clip):
        return (i + (clip >> 1)) & 1

    def pack(a):
        def group(s, _):
            for hg in range(4):
                for t in range(12):
                    b, m = divmod(t, 3)
                    rows = pl.ds(pl.multiple_of(64 * b + 16 * s, 16), 16)
                    lanes = pl.ds((3 * hg + m) * HD, HD)
                    dev = 2 * (4 * s + hg) + lax.rem(t + core, 2)
                    xs[a, half_of(t // 2, c), dev, t // 4] = inp[a, rows, lanes]
            return 0

        lax.fori_loop(0, 4, group, 0)

    def x_send(src, dst, i):
        def one(d, _):
            other = d >= 15
            e = jnp.where(other, d - 15, jnp.where(d >= 10, d + 1, d))
            row, col = lax.rem(e // 4 + 2 + c // 8, 4), lax.rem(lax.rem(e, 4) + 2 + lax.rem(c // 2, 4), 4)
            dev = 8 * row + 2 * col + lax.rem(core + jnp.where(other, 1, 0), 2)
            pltpu.make_async_remote_copy(
                src_ref=src.at[dev], dst_ref=dst.at[c], send_sem=xss.at[i], recv_sem=xrs.at[i],
                device_id={"grp": dev}, device_id_type=MESH,
            ).start()
            return 0

        lax.fori_loop(0, 31, one, 0)
        pltpu.make_async_copy(src.at[c], dst.at[c], xls.at[i]).start()

    def x_wait(src, dst, i):
        part = dst.at[pl.ds(0, 31)]
        pltpu.make_async_copy(part, part, xrs.at[i]).wait()
        pltpu.make_async_copy(src.at[c], dst.at[c], xls.at[i]).wait()

    def x_drain(src, i):
        part = src.at[pl.ds(0, 31)]
        pltpu.make_async_copy(part, part, xss.at[i]).wait()

    loads[0].wait()
    pack(0)
    pl.semaphore_wait(barrier, 46)
    for h in range(2):
        x_send(xs.at[0, h], xr[h][0], h)
    loads[1].wait()
    pack(1)
    for h in range(2):
        x_send(xs.at[1, h], xr[h][1], 2 + h)

    row = lax.broadcasted_iota(jnp.int32, table.shape[2:], 0)
    lane = lax.broadcasted_iota(jnp.int32, table.shape[2:], 1)
    place = 128 * row + lane
    zero = jnp.int32(0)
    for h in range(2):

        def count_units(clip, sums):
            frames = shape_ref[0, clip]
            count = (3 * (shape_ref[1, clip] >> 6) + 1 - ((core + clip) & 1)) >> 1
            count = (count + 1 - ((h + (clip >> 1)) & 1)) >> 1
            units[h, clip] = count
            is16, is8 = frames == 16, frames == 8
            first[h, clip] = jnp.where(is16, sums[0], jnp.where(is8, sums[1], sums[2]))
            return (
                sums[0] + jnp.where(is16, count, 0),
                sums[1] + jnp.where(is8, count, 0),
                sums[2] + jnp.where(is16 | is8, 0, count),
            )

        n16, n8, _ = lax.fori_loop(0, 32, count_units, (zero, zero, zero))

        def find_slots(clip, found):
            unit, count = found
            frames = shape_ref[0, clip]
            start = first[h, clip] + jnp.where(frames == 16, 0, jnp.where(frames == 8, n16, n16 + n8))
            first[h, clip] = start
            inner = place - start
            hit = (inner >= 0) & (inner < units[h, clip])
            return jnp.where(hit, inner + 3 * clip, unit), jnp.where(hit, frames, count)

        unit, count = lax.fori_loop(0, 32, find_slots, (jnp.zeros_like(place), jnp.full_like(place, 16)))
        table[h, 0] = unit
        table[h, 1] = count
    to_smem = pltpu.make_async_copy(table, slot_ref, tab_sem.at[0])
    to_smem.start()

    row_id = lax.broadcasted_iota(jnp.int32, (256, 256), 0)
    col_id = lax.broadcasted_iota(jnp.int32, (256, 256), 1)
    for i in range(3):
        period = 16 * 2**i
        same = (row_id & (period - 1)) == (col_id & (period - 1))
        bias[i] = jnp.where(same, 0.0, NEG)
    for h in range(2):
        zr[h][total] = jnp.zeros((TILE, HD), jnp.bfloat16)

    for i in (2, 3, 4):
        loads[i].wait()
    scale = HD ** (-0.5)
    lane_id = lax.broadcasted_iota(jnp.int32, (1, 256), 1)
    key_bias = jnp.where(lane_id < shape_ref[1, c], 0.0, NEG)

    def heads(hg, _):
        for m in range(3):
            lanes = pl.ds(pl.multiple_of((3 * hg + m) * HD, HD), HD)
            scores = nt_dot(inp[2, :, lanes], inp[3, :, lanes]) * scale + key_bias
            weights = softmax_weights(scores)
            out = jnp.dot(weights, inp[4, :, lanes], preferred_element_type=jnp.float32)
            out = out.astype(jnp.bfloat16)
            for b in range(4):
                t = 3 * b + m
                for s in range(4):
                    dev = 2 * (4 * s + hg) + lax.rem(t + core, 2)
                    xs[2, half_of(t // 2, c), dev, t // 4] = out[64 * b + 16 * s : 64 * b + 16 * s + 16]
        return 0

    lax.fori_loop(0, 4, heads, 0)
    for h in range(2):
        x_send(xs.at[2, h], xr[h][2], 4 + h)
    to_smem.wait()

    class Ring:
        def __init__(self, half, kind, send, land, back):
            self.half, self.kind, self.sources, self.sem = half, kind, 16 >> kind, 12 * half + kind
            self.send, self.land, self.back = send, land, back
            self.start, self.count, self.slots = plan[kind]
            self.off = capacity(plan)[kind] - self.count * self.slots
            self.place = lax.rem(z - self.start + 16, 16)
            self.works = self.place < self.count

    halves = [[Ring(h, kind, *exchange[h][3 * kind : 3 * kind + 3]) for kind in range(3)] for h in range(2)]

    def entry(half, kind, r):
        return slot_ref[half, kind, r >> 7, r & 127]

    def on_sources(ring, run):
        if ring.sources == 16:
            run()
        else:
            pl.when(z < ring.sources)(run)

    def z_send(a, ring):
        i = 3 * a + ring.sem

        def one(d, _):
            j = lax.rem(z + d, ring.count)
            dev = lax.rem(ring.start + j, 16)
            for k in range(ring.slots):
                index = entry(ring.half, 0, ring.off + j * ring.slots + k)
                ring.send[a, j, k] = xr[ring.half][a][index // 3, lax.rem(index, 3)]

            @pl.when(dev != z)
            def _():
                pltpu.make_async_remote_copy(
                    src_ref=ring.send.at[a, j], dst_ref=ring.land.at[a, z], send_sem=zss.at[i], recv_sem=zrs.at[i],
                    device_id={"seq": dev}, device_id_type=MESH,
                ).start()

            @pl.when(dev == z)
            def _():
                pltpu.make_async_copy(ring.send.at[a, j], ring.land.at[a, z], zls.at[i]).start()

            return 0

        lax.fori_loop(0, ring.count, one, 0)

    def z_sent(a, ring):
        i = 3 * a + ring.sem
        for mine in (0, 1):
            if ring.count > mine:

                @pl.when(ring.works if mine else jnp.logical_not(ring.works))
                def _():
                    part = ring.send.at[a, pl.ds(0, ring.count - mine)]
                    pltpu.make_async_copy(part, part, zss.at[i]).wait()

    def z_wait(a, ring):
        i = 3 * a + ring.sem
        part = ring.land.at[a, pl.ds(0, ring.sources - 1)]
        pltpu.make_async_copy(part, part, zrs.at[i]).wait()
        one = ring.land.at[a, 0]
        pltpu.make_async_copy(one, one, zls.at[i]).wait()

    for a in range(3):
        for h in range(2):
            x_wait(xs.at[a, h], xr[h][a], 2 * a + h)
            for ring in halves[h]:
                on_sources(ring, functools.partial(z_send, a, ring))

    def trace(group):
        for b in reversed(range(5)):
            low = group & (31 - (1 << b))
            group = group ^ (((route_ref[low] >> b) & 1) << b)
        return group

    def route_units(group, _):
        clip = trace(group)
        for h in range(2):
            start = first[h, clip]
            count = jnp.where(z < shape_ref[0, clip], units[h, clip], 0)
            for i in range(3):
                out_tab[h, group * 3 + i] = jnp.where(i < count, start + i, total)
        return 0

    lax.fori_loop(0, 32, route_units, 0)

    for ring in halves[0] + halves[1]:
        step = 16 // ring.sources
        ring.blocks = [(k, min(step, ring.slots - k), k // step) for k in range(0, ring.slots, step)]

    def block(ring, a, k, n):
        return ring.land[a, :, k : k + n].reshape(ring.sources * n * TILE, HD)

    def z_weights(ring):
        for a in range(2):
            z_wait(a, ring)
        for k, n, at in ring.blocks:
            rows = ring.sources * n * TILE
            scores = nt_dot(block(ring, 1, k, n), block(ring, 0, k, n)) * scale
            which = {1: 0, 2: 1, 4: 2}.get(n)
            if which is None:
                r = lax.broadcasted_iota(jnp.int32, (rows, rows), 0)
                q = lax.broadcasted_iota(jnp.int32, (rows, rows), 1)
                scores = jnp.where(lax.rem(r, n * TILE) == lax.rem(q, n * TILE), scores, NEG)
            else:
                scores = scores + bias[which, :rows, :rows]
            if ring.kind < 2:
                lane = lax.broadcasted_iota(jnp.int32, (1, rows), 1)
                frame = lane // (n * TILE)
                spot = ring.off + ring.place * ring.slots + k
                count = entry(ring.half, 1, spot)
                if n == 2:
                    count = jnp.where((lane // TILE) % 2 == 0, count, entry(ring.half, 1, spot + 1))
                scores = scores + jnp.where(frame < count, 0.0, NEG)
            wts[ring.half, ring.kind, at, :rows, :rows] = softmax_weights(scores)

    def z_values(ring):
        z_wait(2, ring)
        for k, n, at in ring.blocks:
            rows = ring.sources * n * TILE
            out = jnp.dot(
                wts[ring.half, ring.kind, at, :rows, :rows], block(ring, 2, k, n), preferred_element_type=jnp.float32
            ).astype(jnp.bfloat16)
            out = out.reshape(ring.sources, n, TILE, HD)
            for j in range(n):
                ring.back[:, k + j] = out[:, j]
        i = 9 + ring.sem
        home = zr[ring.half].at[pl.ds(ring.off + ring.place * ring.slots, ring.slots)]

        def one(d, _):
            dev = lax.rem(z + d, ring.sources)
            pltpu.make_async_remote_copy(
                src_ref=ring.back.at[dev], dst_ref=home, send_sem=zss.at[i], recv_sem=zrs.at[i],
                device_id={"seq": dev}, device_id_type=MESH,
            ).start()
            return 0

        lax.fori_loop(1, ring.sources, one, 0)
        pltpu.make_async_copy(ring.back.at[z], home, zls.at[i]).start()

    def z_home(ring):
        i = 9 + ring.sem
        for mine in (0, 1):

            @pl.when(ring.works if mine else jnp.logical_not(ring.works))
            def _():
                if ring.count > mine:
                    part = zr[ring.half].at[pl.ds(ring.off, (ring.count - mine) * ring.slots)]
                    pltpu.make_async_copy(part, part, zrs.at[i]).wait()
                if mine:
                    one = ring.back.at[0]
                    pltpu.make_async_copy(one, one, zls.at[i]).wait()

    def z_returned(ring):
        part = ring.back.at[pl.ds(0, ring.sources - 1)]
        pltpu.make_async_copy(part, part, zss.at[9 + ring.sem]).wait()

    for rings in halves:
        for ring in rings:
            pl.when(ring.works)(functools.partial(z_weights, ring))
        for ring in rings:
            pl.when(ring.works)(functools.partial(z_values, ring))

    for h in range(2):
        for ring in halves[h]:
            on_sources(ring, functools.partial(z_home, ring))

        def collect(dev, _):
            for i in range(3):
                xso[h, dev, i] = zr[h][out_tab[h, dev * 3 + i]]
            return 0

        lax.fori_loop(0, 32, collect, 0)
        x_send(xso.at[h], xro.at[h], 6 + h)
    for h in range(2):
        x_wait(xso.at[h], xro.at[h], 6 + h)
    clip = trace(c)

    def place_out(s, _):
        for hg in range(4):
            for t in range(12):
                b, m = divmod(t, 3)
                rows = pl.ds(pl.multiple_of(64 * b + 16 * s, 16), 16)
                dev = 2 * (4 * s + hg) + ((t + clip) & 1)
                o_ref[0, 0, rows, (3 * hg + m) * HD : (3 * hg + m + 1) * HD] = xro[half_of(t // 2, clip), dev, t // 4]
        return 0

    lax.fori_loop(0, 4, place_out, 0)
    for h in range(2):
        for a in range(3):
            x_drain(xs.at[a, h], 2 * a + h)
        x_drain(xso.at[h], 6 + h)
        for ring in halves[h]:
            for a in range(3):
                on_sources(ring, functools.partial(z_sent, a, ring))
            pl.when(ring.works)(functools.partial(z_returned, ring))


def packed(cid, plan, clip_shape, route, arrays):
    total = capacity(plan)[-1]
    rows = (total + 1023) // 1024 * 8
    bf = jnp.bfloat16
    smem = pl.BlockSpec(memory_space=pltpu.SMEM)
    exchange = []
    for sources, (_, count, slots) in zip((16, 8, 4), plan):
        exchange.append(pltpu.VMEM((3, count, slots, TILE, HD), bf))
        exchange.append(pltpu.VMEM((3, sources, slots, TILE, HD), bf))
        exchange.append(pltpu.VMEM((sources, slots, TILE, HD), bf))
    n_blocks = max(-(-slots // (16 // sources)) for sources, (_, _, slots) in zip((16, 8, 4), plan))
    return pl.pallas_call(
        functools.partial(kernel, plan),
        out_shape=jax.ShapeDtypeStruct(arrays[0].shape, bf),
        in_specs=[smem] * 2 + [pl.BlockSpec(memory_space=pl.ANY)] * 5,
        out_specs=pl.BlockSpec(memory_space=pltpu.VMEM),
        scratch_shapes=[
            pltpu.VMEM((5, 256, 12 * HD), bf),
            pltpu.VMEM((3, 2, 32, 3, TILE, HD), bf),
            *[pltpu.VMEM((32, 3, TILE, HD), bf)] * 6,
            *exchange,
            *exchange,
            pltpu.VMEM((2, 3, n_blocks, 256, 256), bf),
            pltpu.VMEM((3, 256, 256), jnp.float32),
            pltpu.VMEM((total + 1, TILE, HD), bf),
            pltpu.VMEM((total + 1, TILE, HD), bf),
            pltpu.VMEM((2, 32, 3, TILE, HD), bf),
            pltpu.VMEM((2, 32, 3, TILE, HD), bf),
            pltpu.VMEM((2, 2, rows, 128), jnp.int32),
            pltpu.SMEM((2, 2, rows, 128), jnp.int32),
            pltpu.SMEM((2, 32), jnp.int32),
            pltpu.SMEM((2, 32), jnp.int32),
            pltpu.SMEM((2, 96), jnp.int32),
            pltpu.SemaphoreType.DMA((5,)),
            *[pltpu.SemaphoreType.DMA((8,))] * 3,
            *[pltpu.SemaphoreType.DMA((24,))] * 3,
            pltpu.SemaphoreType.DMA((1,)),
        ],
        compiler_params=pltpu.CompilerParams(
            collective_id=cid, has_side_effects=True, vmem_limit_bytes=56 * 1024 * 1024
        ),
    )(clip_shape, route, *arrays)


def plan_of(clip_shape):
    frames, patches = clip_shape.T[:1], clip_shape.T[1:]
    kind = jnp.arange(12, dtype=jnp.int32)[:, None]
    clips = jnp.arange(32, dtype=jnp.int32)[None, :]
    units = (3 * (patches >> 6) + 1 - ((kind + clips) & 1)) >> 1
    units = (units + 1 - (((kind >> 1) + (clips >> 1)) & 1)) >> 1
    needed = jnp.sum(jnp.where(frames >= (16 >> (kind >> 2)), units, 0), axis=1)
    over = 0
    for plan in PLANS:
        a, b, d = capacity(plan)
        at = jnp.arange(12, dtype=jnp.int32) >> 2
        held = jnp.where(at == 0, a, jnp.where(at == 1, b, d))
        over = over + (needed > held).astype(jnp.int32)
    return jnp.max(over)


def body(query_sp, key_sp, value_sp, query_tm, key_tm, clip_shape, route):
    choice = plan_of(clip_shape)

    def run(i, *args):
        arrays, (shape, way) = args[:5], args[5:]
        return packed(i, PLANS[i], shape.T, way, arrays)

    branches = [functools.partial(run, i) for i in range(len(PLANS))] + [general]
    return lax.switch(
        choice, branches, query_sp, key_sp, value_sp, query_tm, key_tm, clip_shape, route
    )


def solution(mesh):
    in_specs = (
        P("grp", "seq", None, None),
        P("grp", "seq", None, None),
        P("grp", "seq", None, None),
        P("grp", "seq", None, None),
        P("grp", "seq", None, None),
        P(),
        P(),
    )
    out_specs = P("grp", "seq", None, None)
    return jax.shard_map(body, mesh=mesh, in_specs=in_specs, out_specs=out_specs, check_vma=False)
```

```python
import functools

import jax
import jax.numpy as jnp
from jax import lax
from jax.experimental import pallas as pl
from jax.experimental.pallas import tpu as pltpu
from jax.sharding import PartitionSpec as P

HD = 128
TILE = 16
MESH = pl.DeviceIdType.MESH
NEG = -1e30
PLANS = (
    ((6, 12, 2), (3, 2, 10), (1, 2, 11)),
    ((6, 12, 3), (3, 2, 9), (2, 1, 18)),
    ((5, 14, 3), (3, 2, 11), (1, 2, 8)),
)


def capacity(plan):
    sums = []
    for _, count, slots in plan:
        sums.append(count * slots + (sums[-1] if sums else 0))
    return sums


def swapped(value, axis, bit):
    mask = 2**bit
    pairs = [(source, source ^ mask) for source in range(lax.axis_size(axis))]
    return lax.ppermute(value, axis, pairs)


def softmax_rows(scores):
    top = jnp.max(scores, axis=-1, keepdims=True)
    expo = jnp.exp(scores - top)
    return expo / jnp.sum(expo, axis=-1, keepdims=True)


def section_cross(route, group_idx, section):
    partner = jnp.bitwise_xor(group_idx, 1 << section)
    lower = jnp.minimum(group_idx, partner)
    return jnp.bitwise_and(jnp.right_shift(route[lower], section), 1) == 1


def general(query_sp, key_sp, value_sp, query_tm, key_tm, clip_shape, route):
    groups = lax.axis_size("grp")
    shards = lax.axis_size("seq")
    group_idx = lax.axis_index("grp")
    shard_idx = lax.axis_index("seq")
    sections = groups.bit_length() - 1
    frames_dev = query_sp.shape[1]
    patches = query_sp.shape[2]
    width = query_sp.shape[3]
    heads = width // HD
    frames = frames_dev * shards
    patches_dev = patches // shards
    scale = HD ** (-0.5)
    own_shape = clip_shape[group_idx]
    frame_ids = shard_idx * frames_dev + jnp.arange(frames_dev, dtype=jnp.int32)
    patch_all = jnp.arange(patches, dtype=jnp.int32)
    shaped = (frames_dev, patches, heads, HD)
    queries = query_sp[0].reshape(shaped)
    keys = key_sp[0].reshape(shaped)
    values = value_sp[0].reshape(shaped)
    scores = (
        jnp.einsum("fphd,fqhd->fhpq", queries, keys, preferred_element_type=jnp.float32) * scale
    )
    scores = jnp.where(patch_all[None, None, None, :] < own_shape[1], scores, NEG)
    weights = softmax_rows(scores).astype(jnp.bfloat16)
    spatial = jnp.einsum("fhpq,fqhd->fphd", weights, values, preferred_element_type=jnp.float32)
    valid_sp = (frame_ids[:, None] < own_shape[0]) & (patch_all[None, :] < own_shape[1])
    spatial = jnp.where(valid_sp[:, :, None, None], spatial, 0.0).astype(jnp.bfloat16)
    spatial = spatial.reshape(1, frames_dev, patches, width)
    query_pt, key_pt, spatial_pt = (
        lax.all_to_all(query_tm, "seq", split_axis=2, concat_axis=1, tiled=True),
        lax.all_to_all(key_tm, "seq", split_axis=2, concat_axis=1, tiled=True),
        lax.all_to_all(spatial, "seq", split_axis=2, concat_axis=1, tiled=True),
    )
    frame_all = jnp.arange(frames, dtype=jnp.int32)
    patch_ids = shard_idx * patches_dev + jnp.arange(patches_dev, dtype=jnp.int32)
    shaped_tm = (frames, patches_dev, heads, HD)
    queries_tm = query_pt[0].reshape(shaped_tm)
    keys_tm = key_pt[0].reshape(shaped_tm)
    values_tm = spatial_pt[0].reshape(shaped_tm)
    scores_tm = (
        jnp.einsum("fphd,gphd->phfg", queries_tm, keys_tm, preferred_element_type=jnp.float32)
        * scale
    )
    scores_tm = jnp.where(frame_all[None, None, None, :] < own_shape[0], scores_tm, NEG)
    weights_tm = softmax_rows(scores_tm).astype(jnp.bfloat16)
    temporal = jnp.einsum(
        "phfg,gphd->fphd", weights_tm, values_tm, preferred_element_type=jnp.float32
    )
    valid_tm = (frame_all[:, None] < own_shape[0]) & (patch_ids[None, :] < own_shape[1])
    temporal = jnp.where(valid_tm[:, :, None, None], temporal, 0.0).astype(jnp.bfloat16)
    temporal = temporal.reshape(1, frames, patches_dev, width)
    result = lax.all_to_all(temporal, "seq", split_axis=1, concat_axis=2, tiled=True)
    for section in range(sections):
        other = swapped(result, "grp", section)
        result = jnp.where(section_cross(route, group_idx, section), other, result)
    return result


def softmax_weights(scores):
    top = jnp.max(scores, axis=-1, keepdims=True)
    expo = jnp.exp(scores - top)
    return (expo * (1.0 / jnp.sum(expo, axis=-1, keepdims=True))).astype(jnp.bfloat16)


def nt_dot(a, b):
    return lax.dot_general(a, b, (((1,), (1,)), ((), ())), preferred_element_type=jnp.float32)


def kernel(
    plan, shape_ref, route_ref,
    q_hbm, k_hbm, v_hbm, qt_hbm, kt_hbm, o_ref,
    inp, xs, *refs,
):
    total = capacity(plan)[-1]
    xr, refs = (refs[0:3], refs[3:6]), refs[6:]
    exchange, refs = (refs[0:9], refs[9:18]), refs[18:]
    wts, bias, zr0, zr1, xso, xro, table, slot_ref, first, units, out_tab, *refs = refs
    in_sem, xss, xrs, xls, zss, zrs, zls, tab_sem = refs
    zr = (zr0, zr1)
    c = lax.axis_index("grp")
    z = lax.axis_index("seq")
    core = lax.rem(c, 2)
    barrier = pltpu.get_barrier_semaphore()

    def greet_x(d, _):
        pl.semaphore_signal(barrier, inc=1, device_id={"grp": lax.rem(c + d, 32)}, device_id_type=MESH)
        return 0

    def greet_z(d, _):
        pl.semaphore_signal(barrier, inc=1, device_id={"seq": lax.rem(z + d, 16)}, device_id_type=MESH)
        return 0

    lax.fori_loop(1, 16, greet_z, 0)
    lax.fori_loop(1, 32, greet_x, 0)

    loads = [
        pltpu.make_async_copy(ref.at[0, 0], inp.at[i], in_sem.at[i])
        for i, ref in enumerate((kt_hbm, qt_hbm, q_hbm, k_hbm, v_hbm))
    ]
    for load in loads:
        load.start()

    def half_of(i, clip):
        return (i + (clip >> 1)) & 1

    def pack(a):
        def group(s, _):
            for hg in range(4):
                for t in range(12):
                    b, m = divmod(t, 3)
                    rows = pl.ds(pl.multiple_of(64 * b + 16 * s, 16), 16)
                    lanes = pl.ds((3 * hg + m) * HD, HD)
                    dev = 2 * (4 * s + hg) + lax.rem(t + core, 2)
                    xs[a, half_of(t // 2, c), dev, t // 4] = inp[a, rows, lanes]
            return 0

        lax.fori_loop(0, 4, group, 0)

    def x_send(src, dst, i):
        def one(d, _):
            other = d >= 15
            e = jnp.where(other, d - 15, jnp.where(d >= 10, d + 1, d))
            row, col = lax.rem(e // 4 + 2 + c // 8, 4), lax.rem(lax.rem(e, 4) + 2 + lax.rem(c // 2, 4), 4)
            dev = 8 * row + 2 * col + lax.rem(core + jnp.where(other, 1, 0), 2)
            pltpu.make_async_remote_copy(
                src_ref=src.at[dev], dst_ref=dst.at[c], send_sem=xss.at[i], recv_sem=xrs.at[i],
                device_id={"grp": dev}, device_id_type=MESH,
            ).start()
            return 0

        lax.fori_loop(0, 31, one, 0)
        pltpu.make_async_copy(src.at[c], dst.at[c], xls.at[i]).start()

    def x_wait(src, dst, i):
        part = dst.at[pl.ds(0, 31)]
        pltpu.make_async_copy(part, part, xrs.at[i]).wait()
        pltpu.make_async_copy(src.at[c], dst.at[c], xls.at[i]).wait()

    def x_drain(src, i):
        part = src.at[pl.ds(0, 31)]
        pltpu.make_async_copy(part, part, xss.at[i]).wait()

    loads[0].wait()
    pack(0)
    pl.semaphore_wait(barrier, 46)
    for h in range(2):
        x_send(xs.at[0, h], xr[h][0], h)
    row = lax.broadcasted_iota(jnp.int32, table.shape[2:], 0)
    lane = lax.broadcasted_iota(jnp.int32, table.shape[2:], 1)
    place = 128 * row + lane
    zero = jnp.int32(0)
    for h in range(2):

        def count_units(clip, sums):
            frames = shape_ref[0, clip]
            count = (3 * (shape_ref[1, clip] >> 6) + 1 - ((core + clip) & 1)) >> 1
            count = (count + 1 - ((h + (clip >> 1)) & 1)) >> 1
            units[h, clip] = count
            is16, is8 = frames == 16, frames == 8
            first[h, clip] = jnp.where(is16, sums[0], jnp.where(is8, sums[1], sums[2]))
            return (
                sums[0] + jnp.where(is16, count, 0),
                sums[1] + jnp.where(is8, count, 0),
                sums[2] + jnp.where(is16 | is8, 0, count),
            )

        n16, n8, _ = lax.fori_loop(0, 32, count_units, (zero, zero, zero))

        def find_slots(clip, found):
            unit, count = found
            frames = shape_ref[0, clip]
            start = first[h, clip] + jnp.where(frames == 16, 0, jnp.where(frames == 8, n16, n16 + n8))
            first[h, clip] = start
            inner = place - start
            hit = (inner >= 0) & (inner < units[h, clip])
            return jnp.where(hit, inner + 3 * clip, unit), jnp.where(hit, frames, count)

        unit, count = lax.fori_loop(0, 32, find_slots, (jnp.zeros_like(place), jnp.full_like(place, 16)))
        table[h, 0] = unit
        table[h, 1] = count
    to_smem = pltpu.make_async_copy(table, slot_ref, tab_sem.at[0])
    to_smem.start()

    loads[1].wait()
    pack(1)
    for h in range(2):
        x_send(xs.at[1, h], xr[h][1], 2 + h)

    class Ring:
        def __init__(self, half, kind, send, land, back):
            self.half, self.kind, self.sources, self.sem = half, kind, 16 >> kind, 12 * half + kind
            self.send, self.land, self.back = send, land, back
            self.start, self.count, self.slots = plan[kind]
            self.off = capacity(plan)[kind] - self.count * self.slots
            self.place = lax.rem(z - self.start + 16, 16)
            self.works = self.place < self.count

    halves = [[Ring(h, kind, *exchange[h][3 * kind : 3 * kind + 3]) for kind in range(3)] for h in range(2)]

    def entry(half, kind, r):
        return slot_ref[half, kind, r >> 7, r & 127]

    def on_sources(ring, run):
        if ring.sources == 16:
            run()
        else:
            pl.when(z < ring.sources)(run)

    def z_send(a, ring):
        i = 3 * a + ring.sem

        def one(d, _):
            j = lax.rem(z + d, ring.count)
            dev = lax.rem(ring.start + j, 16)
            for k in range(ring.slots):
                index = entry(ring.half, 0, ring.off + j * ring.slots + k)
                ring.send[a, j, k] = xr[ring.half][a][index // 3, lax.rem(index, 3)]

            @pl.when(dev != z)
            def _():
                pltpu.make_async_remote_copy(
                    src_ref=ring.send.at[a, j], dst_ref=ring.land.at[a, z], send_sem=zss.at[i], recv_sem=zrs.at[i],
                    device_id={"seq": dev}, device_id_type=MESH,
                ).start()

            @pl.when(dev == z)
            def _():
                pltpu.make_async_copy(ring.send.at[a, j], ring.land.at[a, z], zls.at[i]).start()

            return 0

        lax.fori_loop(0, ring.count, one, 0)

    def z_sent(a, ring):
        i = 3 * a + ring.sem
        for mine in (0, 1):
            if ring.count > mine:

                @pl.when(ring.works if mine else jnp.logical_not(ring.works))
                def _():
                    part = ring.send.at[a, pl.ds(0, ring.count - mine)]
                    pltpu.make_async_copy(part, part, zss.at[i]).wait()

    def z_wait(a, ring):
        i = 3 * a + ring.sem
        part = ring.land.at[a, pl.ds(0, ring.sources - 1)]
        pltpu.make_async_copy(part, part, zrs.at[i]).wait()
        one = ring.land.at[a, 0]
        pltpu.make_async_copy(one, one, zls.at[i]).wait()

    def pass_on(a):
        for h in range(2):
            x_wait(xs.at[a, h], xr[h][a], 2 * a + h)
            for ring in halves[h]:
                on_sources(ring, functools.partial(z_send, a, ring))

    to_smem.wait()
    pass_on(0)

    row_id = lax.broadcasted_iota(jnp.int32, (256, 256), 0)
    col_id = lax.broadcasted_iota(jnp.int32, (256, 256), 1)
    for i in range(3):
        period = 16 * 2**i
        same = (row_id & (period - 1)) == (col_id & (period - 1))
        bias[i] = jnp.where(same, 0.0, NEG)
    for h in range(2):
        zr[h][total] = jnp.zeros((TILE, HD), jnp.bfloat16)

    for i in (2, 3, 4):
        loads[i].wait()
    scale = HD ** (-0.5)
    lane_id = lax.broadcasted_iota(jnp.int32, (1, 256), 1)
    key_bias = jnp.where(lane_id < shape_ref[1, c], 0.0, NEG)

    def heads(hg, _):
        for m in range(3):
            lanes = pl.ds(pl.multiple_of((3 * hg + m) * HD, HD), HD)
            scores = nt_dot(inp[2, :, lanes], inp[3, :, lanes]) * scale + key_bias
            weights = softmax_weights(scores)
            out = jnp.dot(weights, inp[4, :, lanes], preferred_element_type=jnp.float32)
            out = out.astype(jnp.bfloat16)
            for b in range(4):
                t = 3 * b + m
                for s in range(4):
                    dev = 2 * (4 * s + hg) + lax.rem(t + core, 2)
                    xs[2, half_of(t // 2, c), dev, t // 4] = out[64 * b + 16 * s : 64 * b + 16 * s + 16]
        return 0

    lax.fori_loop(0, 4, heads, 0)
    for h in range(2):
        x_send(xs.at[2, h], xr[h][2], 4 + h)

    pass_on(1)
    pass_on(2)

    def trace(group):
        for b in reversed(range(5)):
            low = group & (31 - (1 << b))
            group = group ^ (((route_ref[low] >> b) & 1) << b)
        return group

    def route_units(group, _):
        clip = trace(group)
        for h in range(2):
            start = first[h, clip]
            count = jnp.where(z < shape_ref[0, clip], units[h, clip], 0)
            for i in range(3):
                out_tab[h, group * 3 + i] = jnp.where(i < count, start + i, total)
        return 0

    lax.fori_loop(0, 32, route_units, 0)

    for ring in halves[0] + halves[1]:
        step = 16 // ring.sources
        ring.blocks = [(k, min(step, ring.slots - k), k // step) for k in range(0, ring.slots, step)]

    def block(ring, a, k, n):
        return ring.land[a, :, k : k + n].reshape(ring.sources * n * TILE, HD)

    def z_weights(ring):
        for a in range(2):
            z_wait(a, ring)
        for k, n, at in ring.blocks:
            rows = ring.sources * n * TILE
            scores = nt_dot(block(ring, 1, k, n), block(ring, 0, k, n)) * scale
            which = {1: 0, 2: 1, 4: 2}.get(n)
            if which is None:
                r = lax.broadcasted_iota(jnp.int32, (rows, rows), 0)
                q = lax.broadcasted_iota(jnp.int32, (rows, rows), 1)
                scores = jnp.where(lax.rem(r, n * TILE) == lax.rem(q, n * TILE), scores, NEG)
            else:
                scores = scores + bias[which, :rows, :rows]
            if ring.kind < 2:
                lane = lax.broadcasted_iota(jnp.int32, (1, rows), 1)
                frame = lane // (n * TILE)
                spot = ring.off + ring.place * ring.slots + k
                count = entry(ring.half, 1, spot)
                if n == 2:
                    count = jnp.where((lane // TILE) % 2 == 0, count, entry(ring.half, 1, spot + 1))
                scores = scores + jnp.where(frame < count, 0.0, NEG)
            wts[ring.half, ring.kind, at, :rows, :rows] = softmax_weights(scores)

    def z_values(ring):
        z_wait(2, ring)
        for k, n, at in ring.blocks:
            rows = ring.sources * n * TILE
            out = jnp.dot(
                wts[ring.half, ring.kind, at, :rows, :rows], block(ring, 2, k, n), preferred_element_type=jnp.float32
            ).astype(jnp.bfloat16)
            out = out.reshape(ring.sources, n, TILE, HD)
            for j in range(n):
                ring.back[:, k + j] = out[:, j]
        i = 9 + ring.sem
        home = zr[ring.half].at[pl.ds(ring.off + ring.place * ring.slots, ring.slots)]

        def one(d, _):
            dev = lax.rem(z + d, ring.sources)
            pltpu.make_async_remote_copy(
                src_ref=ring.back.at[dev], dst_ref=home, send_sem=zss.at[i], recv_sem=zrs.at[i],
                device_id={"seq": dev}, device_id_type=MESH,
            ).start()
            return 0

        lax.fori_loop(1, ring.sources, one, 0)
        pltpu.make_async_copy(ring.back.at[z], home, zls.at[i]).start()

    def z_home(ring):
        i = 9 + ring.sem
        for mine in (0, 1):

            @pl.when(ring.works if mine else jnp.logical_not(ring.works))
            def _():
                if ring.count > mine:
                    part = zr[ring.half].at[pl.ds(ring.off, (ring.count - mine) * ring.slots)]
                    pltpu.make_async_copy(part, part, zrs.at[i]).wait()
                if mine:
                    one = ring.back.at[0]
                    pltpu.make_async_copy(one, one, zls.at[i]).wait()

    def z_returned(ring):
        part = ring.back.at[pl.ds(0, ring.sources - 1)]
        pltpu.make_async_copy(part, part, zss.at[9 + ring.sem]).wait()

    for rings in halves:
        for ring in rings:
            pl.when(ring.works)(functools.partial(z_weights, ring))
        for ring in rings:
            pl.when(ring.works)(functools.partial(z_values, ring))

    for h in range(2):
        for ring in halves[h]:
            on_sources(ring, functools.partial(z_home, ring))

        def collect(dev, _):
            for i in range(3):
                xso[h, dev, i] = zr[h][out_tab[h, dev * 3 + i]]
            return 0

        lax.fori_loop(0, 32, collect, 0)
        x_send(xso.at[h], xro.at[h], 6 + h)
    for h in range(2):
        x_wait(xso.at[h], xro.at[h], 6 + h)
    clip = trace(c)

    def place_out(s, _):
        for hg in range(4):
            for t in range(12):
                b, m = divmod(t, 3)
                rows = pl.ds(pl.multiple_of(64 * b + 16 * s, 16), 16)
                dev = 2 * (4 * s + hg) + ((t + clip) & 1)
                o_ref[0, 0, rows, (3 * hg + m) * HD : (3 * hg + m + 1) * HD] = xro[half_of(t // 2, clip), dev, t // 4]
        return 0

    lax.fori_loop(0, 4, place_out, 0)
    for h in range(2):
        for a in range(3):
            x_drain(xs.at[a, h], 2 * a + h)
        x_drain(xso.at[h], 6 + h)
        for ring in halves[h]:
            for a in range(3):
                on_sources(ring, functools.partial(z_sent, a, ring))
            pl.when(ring.works)(functools.partial(z_returned, ring))


def packed(cid, plan, clip_shape, route, arrays):
    total = capacity(plan)[-1]
    rows = (total + 1023) // 1024 * 8
    bf = jnp.bfloat16
    smem = pl.BlockSpec(memory_space=pltpu.SMEM)
    exchange = []
    for sources, (_, count, slots) in zip((16, 8, 4), plan):
        exchange.append(pltpu.VMEM((3, count, slots, TILE, HD), bf))
        exchange.append(pltpu.VMEM((3, sources, slots, TILE, HD), bf))
        exchange.append(pltpu.VMEM((sources, slots, TILE, HD), bf))
    n_blocks = max(-(-slots // (16 // sources)) for sources, (_, _, slots) in zip((16, 8, 4), plan))
    return pl.pallas_call(
        functools.partial(kernel, plan),
        out_shape=jax.ShapeDtypeStruct(arrays[0].shape, bf),
        in_specs=[smem] * 2 + [pl.BlockSpec(memory_space=pl.ANY)] * 5,
        out_specs=pl.BlockSpec(memory_space=pltpu.VMEM),
        scratch_shapes=[
            pltpu.VMEM((5, 256, 12 * HD), bf),
            pltpu.VMEM((3, 2, 32, 3, TILE, HD), bf),
            *[pltpu.VMEM((32, 3, TILE, HD), bf)] * 6,
            *exchange,
            *exchange,
            pltpu.VMEM((2, 3, n_blocks, 256, 256), bf),
            pltpu.VMEM((3, 256, 256), jnp.float32),
            pltpu.VMEM((total + 1, TILE, HD), bf),
            pltpu.VMEM((total + 1, TILE, HD), bf),
            pltpu.VMEM((2, 32, 3, TILE, HD), bf),
            pltpu.VMEM((2, 32, 3, TILE, HD), bf),
            pltpu.VMEM((2, 2, rows, 128), jnp.int32),
            pltpu.SMEM((2, 2, rows, 128), jnp.int32),
            pltpu.SMEM((2, 32), jnp.int32),
            pltpu.SMEM((2, 32), jnp.int32),
            pltpu.SMEM((2, 96), jnp.int32),
            pltpu.SemaphoreType.DMA((5,)),
            *[pltpu.SemaphoreType.DMA((8,))] * 3,
            *[pltpu.SemaphoreType.DMA((24,))] * 3,
            pltpu.SemaphoreType.DMA((1,)),
        ],
        compiler_params=pltpu.CompilerParams(
            collective_id=cid, has_side_effects=True, vmem_limit_bytes=56 * 1024 * 1024
        ),
    )(clip_shape, route, *arrays)


def plan_of(clip_shape):
    frames, patches = clip_shape.T[:1], clip_shape.T[1:]
    kind = jnp.arange(12, dtype=jnp.int32)[:, None]
    clips = jnp.arange(32, dtype=jnp.int32)[None, :]
    units = (3 * (patches >> 6) + 1 - ((kind + clips) & 1)) >> 1
    units = (units + 1 - (((kind >> 1) + (clips >> 1)) & 1)) >> 1
    needed = jnp.sum(jnp.where(frames >= (16 >> (kind >> 2)), units, 0), axis=1)
    over = 0
    for plan in PLANS:
        a, b, d = capacity(plan)
        at = jnp.arange(12, dtype=jnp.int32) >> 2
        held = jnp.where(at == 0, a, jnp.where(at == 1, b, d))
        over = over + (needed > held).astype(jnp.int32)
    return jnp.max(over)


def body(query_sp, key_sp, value_sp, query_tm, key_tm, clip_shape, route):
    choice = plan_of(clip_shape)

    def run(i, *args):
        arrays, (shape, way) = args[:5], args[5:]
        return packed(i, PLANS[i], shape.T, way, arrays)

    branches = [functools.partial(run, i) for i in range(len(PLANS))] + [general]
    return lax.switch(
        choice, branches, query_sp, key_sp, value_sp, query_tm, key_tm, clip_shape, route
    )


def solution(mesh):
    in_specs = (
        P("grp", "seq", None, None),
        P("grp", "seq", None, None),
        P("grp", "seq", None, None),
        P("grp", "seq", None, None),
        P("grp", "seq", None, None),
        P(),
        P(),
    )
    out_specs = P("grp", "seq", None, None)
    return jax.shard_map(body, mesh=mesh, in_specs=in_specs, out_specs=out_specs, check_vma=False)
```
